32 devices in a mesh: design: 2 (over y), cluster: 4 (over z), blk: 2 (over x), sub: 2 (over core).
Axes of the slice: x: 2, y: 2, z: 4, core: 2. Of those that a mesh axis runs over, the one named last changes fastest.
Arguments:
- density: bfloat16 [16, 256, 256], P(('design', 'cluster')), parts along dimension 0, may hold values from -6 to 6
- far_cols: int32 [256], P(('design', 'cluster', 'blk', 'sub')), parts along dimension 0, may hold values from 0 to 1
- far_bucket: int32 [256], P(('design', 'cluster', 'blk', 'sub')), parts along dimension 0, may hold values from 0 to 4
- far_v: bfloat16 [256, 64, 256], P(('design', 'cluster', 'blk', 'sub')), parts along dimension 0, may hold values from -0.375 to 0.375
- far_u: bfloat16 [256, 64, 256], P(('design', 'cluster', 'blk', 'sub')), parts along dimension 0, may hold values from -0.1875 to 0.1875
- near_rows: int32 [64], P(('design', 'cluster', 'blk', 'sub')), parts along dimension 0, may hold values from 0 to 1
- near_cols: int32 [64], P(('design', 'cluster', 'blk', 'sub')), parts along dimension 0, may hold values from 0 to 5
- near_tiles: bfloat16 [64, 256, 256], P(('design', 'cluster', 'blk', 'sub')), parts along dimension 0, may hold values from -0.125 to 0.125
- ag_leaf: int32 [8192], P(('design', 'cluster', 'blk', 'sub')), parts along dimension 0, may hold values from 0 to 1
- ag_grad: bfloat16 [8192, 3, 256], P(('design', 'cluster', 'blk', 'sub')), parts along dimension 0, may hold values from -0.375 to 0.375
- ag_normal: float32 [6, 4096], P('design', ('cluster', 'blk', 'sub')), parts along dimension 0, may hold values from -5 to 5
- ag_arm: float32 [6, 4096], P('design', ('cluster', 'blk', 'sub')), parts along dimension 0, may hold values from -5 to 5
- ag_area: float32 [8192], P(('design', 'cluster', 'blk', 'sub')), parts along dimension 0, may hold values from 0.002 to 0.02
Outputs:
- potential: bfloat16 [16, 256, 256], P(('design', 'cluster')), parts along dimension 0
- sector_force: float32 [16, 3, 256], P(('design', 'cluster')), parts along dimension 0
- torque: float32 [6, 256], P('design'), parts along dimension 0
The draws below stay inside these ranges and needn't reach their ends.
There are 2 independent parts, one for each index of `design`. The reference program is written for one: setup_inputs(seed, part) draws one part's arguments, and reference() takes and returns one part's arrays. A program takes and returns all parts, laid end to end along the dimension named above; each array names one. Nothing has to cross between parts.
All inputs are finite; a program needn't handle non-finite values.
Results may differ from the reference program's by a relative error of at most 0.0066.
Values may be sent and summed in bfloat16 or wider, within the bound.
A program may use at most 64 MiB of HBM per device.

```python
import math
import jax
import jax.numpy as jnp
from jax import lax

LEAF = 256
R = 64
CL_DEV = 2
NRHS = 256
NEAR_DEV = 2
CLUSTERS = 8
GROUP = 16
FAR_TOTAL = 128
NEAR_TOTAL = 32
AG_TOTAL = 4096
N_CLUSTER = 4
N_BLK = 2
N_SUB = 2


def place_ends(values, stream_key, least, top_value):
    dims = values.shape
    index_at = [jax.random.randint(jax.random.fold_in(stream_key, axis), (), 0, dims[axis]) for axis in range(len(dims))]
    values = values.at[tuple(index_at)].set(least)
    longest = dims.index(max(dims))
    index_at[longest] = (index_at[longest] + 1) % dims[longest]
    return values.at[tuple(index_at)].set(top_value)


def steps_of(stream_key, shape, split, smallest, high):
    gain, own = 1.0, jax.random.fold_in(stream_key, 6)
    for position, parts in split:
        heights = jnp.exp(jax.random.uniform(jax.random.fold_in(own, position), (parts,), jnp.float32, smallest / len(split), high / len(split)))
        gain = gain * jnp.repeat(heights, shape[position] // parts).reshape([-1 if axis == position else 1 for axis in range(len(shape))])
    return gain


def centred(own_key, extent, width, bound, pieces=(), kind=jnp.bfloat16):
    drawn = jax.random.normal(own_key, extent, jnp.float32) * width
    if len(pieces) > 0:
        drawn = steps_of(own_key, extent, pieces, -0.22, 0.18) * drawn
    return jnp.clip(drawn, min=-bound, max=bound).astype(kind)


def setup_inputs(seed: int = 0, part: int = 0) -> dict:
    splits = jax.random.split(jax.random.key(seed), 14)
    part_keys = jax.random.split(jax.random.fold_in(splits[13], part), 14)
    return {
        "density": centred(part_keys[0], (CLUSTERS, LEAF, NRHS), 1.0, 6.0, ((0, 4),)),
        "far_cols": place_ends(jax.random.randint(part_keys[1], (FAR_TOTAL,), 0, CL_DEV), jax.random.fold_in(part_keys[1], 1), 0, CL_DEV - 1).astype(jnp.int32),
        "far_bucket": place_ends(jax.random.randint(part_keys[2], (FAR_TOTAL,), 0, 5), jax.random.fold_in(part_keys[2], 1), 0, 4).astype(jnp.int32),
        "far_v": centred(part_keys[3], (FAR_TOTAL, R, LEAF), LEAF ** -0.5, 0.375, ((0, 16),)),
        "far_u": centred(part_keys[4], (FAR_TOTAL, R, LEAF), (R * GROUP) ** -0.5, 0.1875, ((0, 16),)),
        "near_rows": place_ends(jax.random.randint(part_keys[5], (NEAR_TOTAL,), 0, CL_DEV), jax.random.fold_in(part_keys[5], 1), 0, CL_DEV - 1).astype(jnp.int32),
        "near_cols": place_ends(jax.random.randint(part_keys[6], (NEAR_TOTAL,), 0, 3 * CL_DEV), jax.random.fold_in(part_keys[6], 1), 0, (3 * CL_DEV) - 1).astype(jnp.int32),
        "near_tiles": centred(part_keys[7], (NEAR_TOTAL, LEAF, LEAF), (2 * LEAF * NEAR_DEV * N_BLK * N_SUB // CL_DEV) ** -0.5, 0.125, ((0, 16),)),
        "ag_leaf": place_ends(jax.random.randint(part_keys[8], (AG_TOTAL,), 0, CL_DEV), jax.random.fold_in(part_keys[8], 1), 0, CL_DEV - 1).astype(jnp.int32),
        "ag_grad": centred(part_keys[9], (AG_TOTAL, 3, LEAF), LEAF ** -0.5, 0.375, ((0, 16),)),
        "ag_normal": centred(part_keys[10], (3, AG_TOTAL), 1.0, 5.0, ((1, 16),), jnp.float32),
        "ag_arm": centred(part_keys[11], (3, AG_TOTAL), 1.0, 5.0, ((1, 16),), jnp.float32),
        "ag_area": jnp.clip(jnp.exp(math.log(0.02) - 2.30258502 * jax.random.uniform(part_keys[12], (AG_TOTAL,), jnp.float32) ** steps_of(part_keys[12], (AG_TOTAL,), ((0, 16),), -0.2, 0.2)), 0.002, 0.02),
    }


def rank_table(bucket, rank_dim):
    widths = rank_dim // jnp.left_shift(jnp.int32(1), 4 - bucket) * (bucket > 0).astype(jnp.int32)
    return jnp.arange(rank_dim, dtype=jnp.int32)[None, :] < widths[:, None]

def surface_stress(phi_local, leaf_ids, grad_rows, normals, arms, areas):
    groups, panels, loads = phi_local.shape
    count = leaf_ids.shape[0]
    field_h = jnp.zeros((count, 3, loads), jnp.float32)
    for leaf_idx in range(groups):
        values = jnp.dot(grad_rows.reshape(count * 3, panels), phi_local[leaf_idx], preferred_element_type=jnp.float32)
        field_h = field_h + jnp.where((leaf_ids == leaf_idx)[:, None, None], values.reshape(count, 3, loads), 0.0)
    normal_t = jnp.transpose(normals)[:, :, None]
    along = lax.optimization_barrier(jnp.sum(field_h * normal_t, axis=1))
    squared = lax.optimization_barrier(jnp.sum(field_h * field_h, axis=1))
    traction = along[:, None, :] * field_h - 0.5 * squared[:, None, :] * normal_t
    weighted = traction * areas[:, None, None]
    sectors = jnp.stack([lax.optimization_barrier(jnp.sum(jnp.where((leaf_ids == leaf_idx)[:, None, None], weighted, 0.0), axis=0)) for leaf_idx in range(groups)])
    arm_t = jnp.transpose(arms)[:, :, None]
    moment_x = lax.optimization_barrier(jnp.sum(arm_t[:, 1] * weighted[:, 2] - arm_t[:, 2] * weighted[:, 1], axis=0))
    moment_y = lax.optimization_barrier(jnp.sum(arm_t[:, 2] * weighted[:, 0] - arm_t[:, 0] * weighted[:, 2], axis=0))
    moment_z = lax.optimization_barrier(jnp.sum(arm_t[:, 0] * weighted[:, 1] - arm_t[:, 1] * weighted[:, 0], axis=0))
    return (sectors, jnp.stack([moment_x, moment_y, moment_z]))

def apply_operator(field, far_cols, far_bucket, far_v, far_u, near_rows, near_cols, near_tiles):
    clusters, panels, loads = field.shape
    owners = N_CLUSTER
    per_owner = N_BLK * N_SUB
    rank_dim = far_v.shape[1]
    col_ids = far_cols.reshape(owners, per_owner, clusters) + (jnp.arange(owners, dtype=jnp.int32) * CL_DEV)[:, None, None]
    keep = rank_table(far_bucket, rank_dim).reshape(owners, per_owner, clusters, rank_dim)
    v_all = far_v.reshape(owners, per_owner, clusters, rank_dim, panels)
    u_all = far_u.reshape(owners, per_owner, owners, CL_DEV, rank_dim, panels)

    def one_row(row):
        dest = row // CL_DEV
        within = row % CL_DEV
        v_sel = jnp.take(v_all, row, axis=2).astype(jnp.float32)
        chosen = jnp.take(col_ids, row, axis=2).reshape(-1).astype(jnp.int32)
        x_sel = jnp.take(field, chosen, axis=0).reshape(owners, per_owner, panels, loads).astype(jnp.float32)
        coeffs = jnp.einsum('bkrl,bkln->bkrn', v_sel, x_sel)
        coeffs = jnp.where(jnp.take(keep, row, axis=2)[..., None], coeffs, 0.0).astype(jnp.bfloat16)
        u_sel = jnp.take(jnp.take(u_all, dest, axis=0), within, axis=2).astype(jnp.float32)
        return jnp.einsum('kbrl,bkrn->ln', u_sel, coeffs.astype(jnp.float32))
    far = lax.map(one_row, jnp.arange(clusters, dtype=jnp.int32))
    per_near = near_rows.shape[0] // owners
    near_owner = jnp.arange(near_rows.shape[0], dtype=jnp.int32) // per_near
    rows = (near_owner * CL_DEV + near_rows).astype(jnp.int32)
    cols = ((near_owner * CL_DEV - CL_DEV + near_cols) % clusters).astype(jnp.int32)
    values = jnp.einsum('kij,kjn->kin', near_tiles.astype(jnp.float32), jnp.take(field, cols, axis=0).astype(jnp.float32))
    near = jax.ops.segment_sum(values, rows, num_segments=clusters)
    return (0.5 * field.astype(jnp.float32) + (far + near)).astype(jnp.bfloat16)

def reference(density, far_cols, far_bucket, far_v, far_u, near_rows, near_cols, near_tiles, ag_leaf, ag_grad, ag_normal, ag_arm, ag_area):
    first = apply_operator(density, far_cols, far_bucket, far_v, far_u, near_rows, near_cols, near_tiles)
    potential = apply_operator(first, far_cols, far_bucket, far_v, far_u, near_rows, near_cols, near_tiles)
    loads = potential.shape[2]
    devices_all = N_CLUSTER * N_BLK * N_SUB
    per_owner = N_BLK * N_SUB
    count = ag_leaf.shape[0] // devices_all

    def one_device(index):
        owner = index // per_owner
        phi_local = lax.dynamic_slice_in_dim(potential, (owner * CL_DEV).astype(jnp.int32), CL_DEV, 0)
        start = (index * count).astype(jnp.int32)
        leaf_ids = lax.dynamic_slice_in_dim(ag_leaf, start, count, 0)
        grads = lax.dynamic_slice_in_dim(ag_grad, start, count, 0)
        normals = lax.dynamic_slice_in_dim(ag_normal, start, count, 1)
        arms = lax.dynamic_slice_in_dim(ag_arm, start, count, 1)
        areas = lax.dynamic_slice_in_dim(ag_area, start, count, 0)
        return surface_stress(phi_local, leaf_ids, grads, normals, arms, areas)
    sector_parts, torque_parts = lax.map(one_device, jnp.arange(devices_all, dtype=jnp.int32))
    sector_force = lax.optimization_barrier(jnp.sum(sector_parts.reshape(N_CLUSTER, per_owner, CL_DEV, 3, loads), axis=1)).reshape(N_CLUSTER * CL_DEV, 3, loads)
    torque = lax.optimization_barrier(jnp.sum(torque_parts, axis=0)) / math.sqrt(devices_all)
    return (potential, sector_force, torque)
```

```python
import functools
import math

import jax
import jax.numpy as jnp
from jax import lax
from jax.experimental import pallas as pl
from jax.experimental.pallas import tpu as pltpu
from jax.sharding import PartitionSpec as P

F32 = jnp.float32
BF16 = jnp.bfloat16
LANES = 128


def each(count, body):
    if count <= 4:
        for i in range(count):
            body(i)
    else:
        pl.loop(0, count)(body)


def kernel(
    nc, nb, ns, cl, rank, scale,
    cols_s, bucket_s, nrow_s, ncol_s,
    dens, far_v, far_u, tiles, leaf, grad, normal, arm, area,
    pot_out, sec_out, tor_out,
    vin, vs, vr, vx, u_all, ut, nt, meta, g_v, agrow, agcol, xg1, xg2, cf, part, rs_send, rs_recv,
    pot, stat, stat_r, tor_s, tor_r,
    loc_sem, core_s, core_r, v_s, v_r, vc_s, vc_r,
    z_s, z_r, b_s, b_r, rs_s, rs_r, p_s, p_r, pc_s, pc_r, st_s, st_r, t_s, t_r,
):
    me = lax.axis_index("cluster")
    k = lax.axis_index("blk")
    s = lax.axis_index("sub")
    rows, loads = dens.shape
    panels = rows // cl
    half = loads // ns
    ch = rows // nb
    near = tiles.shape[0]
    vrows = cl * rank
    my_rows = pl.ds(pl.multiple_of(k * ch, ch), ch)
    my_cols = pl.ds(pl.multiple_of(s * half, half), half)
    other = 1 - s

    def rcopy(src, dst, ss, rs, dev):
        return pltpu.make_async_remote_copy(
            src_ref=src, dst_ref=dst, send_sem=ss, recv_sem=rs, device_id=dev,
            device_id_type=pl.DeviceIdType.MESH,
        )

    def zdev(t):
        return {"cluster": t}

    def bdev(t):
        return {"blk": t}

    cdev = {"sub": other}

    local = [
        pltpu.make_async_copy(far_v, vin, loc_sem.at[0]),
        pltpu.make_async_copy(dens.at[:, my_cols], xg1.at[me], loc_sem.at[1]),
        pltpu.make_async_copy(far_u, u_all.at[s], loc_sem.at[2]),
        pltpu.make_async_copy(tiles, nt.at[s], loc_sem.at[3]),
        pltpu.make_async_copy(grad, g_v, loc_sem.at[4]),
    ]
    for c in local:
        c.start()

    bar = pltpu.get_barrier_semaphore()

    def greet_z(d):
        pl.semaphore_signal(
            bar, inc=1, device_id=zdev(lax.rem(me + d + 1, nc)), device_id_type=pl.DeviceIdType.MESH
        )

    each(nc - 1, greet_z)
    mates = [(e, g) for e in range(nb) for g in range(ns) if (e, g) != (0, 0)]
    for e, g in mates:
        pl.semaphore_signal(
            bar, inc=1,
            device_id={"blk": lax.rem(k + e, nb), "sub": lax.rem(s + g, ns)},
            device_id_type=pl.DeviceIdType.MESH,
        )

    rid = lax.broadcasted_iota(jnp.int32, (8, LANES), 0)
    m = jnp.zeros((8, LANES), jnp.int32)
    for i in range(near):
        m = jnp.where(rid == i, ncol_s[i], m)
        m = jnp.where(rid == near + i, nrow_s[i], m)
    meta[pl.ds(s, 1)] = m.astype(F32)[None]

    local[0].wait()
    rr = lax.broadcasted_iota(jnp.int32, (rank, panels), 0)
    hr = lax.broadcasted_iota(jnp.int32, (16, panels), 0)

    def build(a):
        head = jnp.zeros((16, panels), jnp.int32)
        for q in range(cl):
            b = bucket_s[a * cl + q]
            width = jnp.where(b > 0, lax.shift_right_logical(jnp.int32(rank), 4 - b), 0)
            blk = vin[a * cl + q]
            vs[a, q * rank : (q + 1) * rank, :] = jnp.where(
                rr < width, blk.astype(F32), 0.0
            ).astype(BF16)
            head = jnp.where(hr == q, cols_s[a * cl + q], head)
        vs[a, vrows : vrows + 16, :] = head.astype(F32).astype(BF16)

    each(nc, build)

    pl.semaphore_wait(bar, nc - 1 + len(mates))

    def send_x1(d):
        t = lax.rem(me + d + 1, nc)
        rcopy(
            dens.at[my_rows, my_cols], xg1.at[me, my_rows], z_s.at[0, t], z_r.at[0, me], zdev(t)
        ).start()

    each(nc - 1, send_x1)

    def send_v(d):
        t = lax.rem(me + d + 1, nc)
        rcopy(vs.at[t], vr.at[s, me], v_s.at[t], v_r.at[me], zdev(t)).start()

    each(nc - 1, send_v)
    core = [
        rcopy(far_u, u_all.at[s], core_s.at[0], core_r.at[0], cdev),
        rcopy(tiles, nt.at[s], core_s.at[1], core_r.at[1], cdev),
        rcopy(meta.at[s], meta.at[s], core_s.at[2], core_r.at[2], cdev),
    ]
    for c in core:
        c.start()
    rcopy(vs.at[me], vr.at[s, me], vc_s.at[me], vc_r.at[me], cdev).start()

    agrow[0:3, :] = normal[...]
    agrow[3:6, :] = arm[...]
    agrow[6:7, :] = area[...]
    agrow[7:8, :] = leaf[...].astype(F32)
    agcol[...] = jnp.transpose(agrow[...])

    def forward_x(i, xg):
        def body(d):
            c = lax.rem(me + nc - d - 1, nc)
            rcopy(
                xg.at[c, my_rows], xg.at[c, my_rows], z_s.at[i, c], z_r.at[i, c], zdev(c)
            ).wait_recv()
            share(i, xg, c)

        each(nc - 1, body)

    def share(i, xg, c):
        for e in range(1, nb):
            t = lax.rem(k + e, nb)
            rcopy(
                xg.at[c, my_rows], xg.at[c, my_rows], b_s.at[i, c, t], b_r.at[i, c, k], bdev(t)
            ).start()

    def peer_rows(e):
        t = lax.rem(k + nb - e, nb)
        return t, pl.ds(pl.multiple_of(t * ch, ch), ch)

    def wait_shared(i, xg, c):
        for e in range(1, nb):
            t, pr = peer_rows(e)
            rcopy(
                xg.at[c, pr], xg.at[c, pr], b_s.at[i, c, t], b_r.at[i, c, t], bdev(t)
            ).wait_recv()

    forward_x(0, xg1)

    def forward_v(d):
        c = lax.rem(me + nc - d - 1, nc)
        rcopy(vs.at[c], vr.at[s, c], v_s.at[c], v_r.at[c], zdev(c)).wait_recv()
        rcopy(vr.at[s, c], vr.at[s, c], vc_s.at[c], vc_r.at[c], cdev).start()

    each(nc - 1, forward_v)

    local[2].wait()
    core[0].wait_recv()
    group = 4 if nc % 4 == 0 else nc

    for q in range(cl):
        for sp in range(ns):
            def turn(i, q=q, sp=sp):
                u = u_all[sp, pl.ds(i * group, group), q].reshape(group * rank, panels)
                ut[q, sp * (nc // group) + i] = jnp.transpose(u)

            each(nc // group, turn)

    vr[pl.ds(s, 1), pl.ds(me, 1)] = vs[pl.ds(me, 1)][None]

    def expand(d):
        c = lax.rem(me + nc - d, nc)
        rcopy(vs.at[c], vr.at[other, c], vc_s.at[c], vc_r.at[c], cdev).wait_recv()
        for sp in range(ns):
            for q in range(cl):
                v = vr[sp, c, q * rank : (q + 1) * rank, :]
                h = vr[sp, c, vrows : vrows + 16, :][q : q + 1]
                r0 = (sp * cl + q) * rank
                for j in range(cl):
                    w = jnp.where(h.astype(F32) == float(j), 1.0, 0.0).astype(BF16)
                    vx[c, r0 : r0 + rank, j * panels : (j + 1) * panels] = v * w

    each(nc, expand)

    local[1].wait()
    local[3].wait()
    core[1].wait_recv()
    core[2].wait_recv()

    def apply(i, xg):
        def coeff(d):
            c = lax.rem(me + nc - d, nc)
            if i == 0:
                if isinstance(d, int):
                    if d > 0:
                        wait_shared(i, xg, c)
                else:
                    pl.when(d > 0)(lambda: wait_shared(i, xg, c))
            else:
                wait_shared(i, xg, c)
            y = jnp.dot(vx[c], xg[c], preferred_element_type=F32).astype(BF16)
            for sp in range(ns):
                for q in range(cl):
                    r0 = (sp * cl + q) * rank
                    cf[q, sp, c] = y[r0 : r0 + rank]

        each(nc, coeff)
        acc = []
        for q in range(cl):
            total = jnp.zeros((panels, half), F32)
            for sp in range(ns):
                def far_step(gi, total, q=q, sp=sp):
                    w = cf[q, sp, pl.ds(gi * group, group)].reshape(group * rank, half)
                    return total + jnp.dot(
                        ut[q, sp * (nc // group) + gi], w, preferred_element_type=F32
                    )

                if nc == group:
                    total = far_step(0, total)
                else:
                    total = lax.fori_loop(0, nc // group, far_step, total)
            acc.append(total)
        for sp in range(ns):
            for n in range(near):
                col = meta[sp, n : n + 1, :]
                row = meta[sp, near + n : near + n + 1, :]
                chosen = jnp.zeros((panels, half), BF16)
                for j in range(3 * cl):
                    c = lax.rem(me + nc - 1 + j // cl, nc)
                    w = jnp.where(col == float(j), 1.0, 0.0).astype(BF16)
                    p0 = (j % cl) * panels
                    chosen = chosen + xg[c, p0 : p0 + panels, :] * w
                val = jnp.dot(nt[sp, n], chosen, preferred_element_type=F32)
                for q in range(cl):
                    acc[q] = acc[q] + jnp.where(row == float(q), val, 0.0)
        for q in range(cl):
            part[q * panels : (q + 1) * panels, :] = acc[q]
        for e in range(1, nb):
            t = lax.rem(k + e, nb)
            tr = pl.ds(pl.multiple_of(t * ch, ch), ch)
            rs_send[i, e - 1] = part[tr, :].astype(rs_send.dtype)
            rcopy(
                rs_send.at[i, e - 1], rs_recv.at[i, e - 1], rs_s.at[i, e - 1], rs_r.at[i, e - 1], bdev(t)
            ).start()
        out = part[my_rows, :]
        for e in range(1, nb):
            rcopy(
                rs_send.at[i, e - 1], rs_recv.at[i, e - 1], rs_s.at[i, e - 1], rs_r.at[i, e - 1], bdev(k)
            ).wait_recv()
            out = out + rs_recv[i, e - 1].astype(F32)
        return (0.5 * xg[me, my_rows, :].astype(F32) + out).astype(BF16)

    first = apply(0, xg1)
    xg2[me, my_rows, :] = first

    def send_x2(d):
        t = lax.rem(me + d + 1, nc)
        rcopy(
            xg2.at[me, my_rows], xg2.at[me, my_rows], z_s.at[1, t], z_r.at[1, me], zdev(t)
        ).start()

    each(nc - 1, send_x2)
    share(1, xg2, me)
    forward_x(1, xg2)
    potential = apply(1, xg2)

    pot[my_rows, my_cols] = potential
    for e in range(1, nb):
        t = lax.rem(k + e, nb)
        rcopy(
            pot.at[my_rows, my_cols], pot.at[my_rows, my_cols], p_s.at[t], p_r.at[k], bdev(t)
        ).start()
    rcopy(pot.at[my_rows, my_cols], pot.at[my_rows, my_cols], pc_s.at[k], pc_r.at[k], cdev).start()
    for e in range(1, nb):
        t, pr = peer_rows(e)
        rcopy(
            pot.at[pr, my_cols], pot.at[pr, my_cols], p_s.at[t], p_r.at[t], bdev(t)
        ).wait_recv()
        rcopy(pot.at[pr, my_cols], pot.at[pr, my_cols], pc_s.at[t], pc_r.at[t], cdev).start()
    oc = pl.ds(pl.multiple_of(other * half, half), half)
    for e in range(nb):
        t, pr = peer_rows(e)
        rcopy(pot.at[pr, oc], pot.at[pr, oc], pc_s.at[t], pc_r.at[t], cdev).wait_recv()
    pot_copy = pltpu.make_async_copy(pot, pot_out, loc_sem.at[5])
    pot_copy.start()

    local[4].wait()
    count = g_v.shape[1]
    step = 64

    def stress(gi, acc):
        g0 = pl.multiple_of(gi * step, step)
        cols = agcol[pl.ds(g0, step), :]
        n = [cols[:, j : j + 1] for j in range(3)]
        a = [cols[:, 3 + j : 4 + j] for j in range(3)]
        ar = cols[:, 6:7]
        lf = cols[:, 7:8]
        field = []
        for j in range(3):
            g = g_v[j, pl.ds(g0, step), :]
            fj = jnp.zeros((step, loads), F32)
            for q in range(cl):
                v = jnp.dot(g, pot[q * panels : (q + 1) * panels, :], preferred_element_type=F32)
                fj = jnp.where(lf == float(q), v, fj)
            field.append(fj)
        along = field[0] * n[0] + field[1] * n[1] + field[2] * n[2]
        sq = 0.5 * (field[0] * field[0] + field[1] * field[1] + field[2] * field[2])
        w = [(along * field[j] - sq * n[j]) * ar for j in range(3)]
        terms = []
        for q in range(cl):
            for j in range(3):
                terms.append(jnp.where(lf == float(q), w[j], 0.0))
        for j in range(3):
            x, y = (j + 1) % 3, (j + 2) % 3
            terms.append(a[x] * w[y] - a[y] * w[x])
        return tuple(
            o + jnp.sum(t.reshape(step // 8, 8, loads), axis=0) for o, t in zip(acc, terms)
        )

    nst = cl * 3 + 3
    zero = tuple(jnp.zeros((8, loads), F32) for _ in range(nst))
    sums = lax.fori_loop(0, count // step, stress, zero)
    for i in range(nst):
        stat[i : i + 1, :] = jnp.sum(sums[i], axis=0, keepdims=True)
    for idx, (e, g) in enumerate(mates):
        rcopy(
            stat, stat_r.at[idx], st_s.at[idx], st_r.at[idx],
            {"blk": lax.rem(k + e, nb), "sub": lax.rem(s + g, ns)},
        ).start()
    tot = stat[0:nst, :]
    for idx in range(len(mates)):
        rcopy(stat, stat_r.at[idx], st_s.at[idx], st_r.at[idx], cdev).wait_recv()
        tot = tot + stat_r[idx, 0:nst, :]
    tor_s[0:3, :] = tot[cl * 3 : cl * 3 + 3]

    def send_t(d):
        t = lax.rem(me + d + 1, nc)
        rcopy(tor_s, tor_r.at[d], t_s.at[d], t_r.at[d], zdev(t)).start()

    each(nc - 1, send_t)
    for q in range(cl):
        sec_out[q] = tot[q * 3 : q * 3 + 3]

    def wait_t(d):
        rcopy(tor_s, tor_r.at[d], t_s.at[d], t_r.at[d], zdev(me)).wait_recv()

    each(nc - 1, wait_t)
    if nc - 1 <= 4:
        tt = tor_s[0:3, :]
        for d in range(nc - 1):
            tt = tt + tor_r[d, 0:3, :]
    else:
        tt = lax.fori_loop(0, nc - 1, lambda d, t: t + tor_r[d, 0:3, :], tor_s[0:3, :])
    tor_out[...] = tt * scale

    def drain_z(d):
        t = lax.rem(me + d + 1, nc)
        rcopy(
            dens.at[my_rows, my_cols], xg1.at[me, my_rows], z_s.at[0, t], z_r.at[0, me], zdev(t)
        ).wait_send()
        rcopy(vs.at[t], vr.at[s, me], v_s.at[t], v_r.at[me], zdev(t)).wait_send()
        rcopy(
            xg2.at[me, my_rows], xg2.at[me, my_rows], z_s.at[1, t], z_r.at[1, me], zdev(t)
        ).wait_send()
        rcopy(tor_s, tor_r.at[d], t_s.at[d], t_r.at[d], zdev(t)).wait_send()
        rcopy(vr.at[s, t], vr.at[s, t], vc_s.at[t], vc_r.at[t], cdev).wait_send()
        for e in range(1, nb):
            b = lax.rem(k + e, nb)
            for i, xg in ((0, xg1), (1, xg2)):
                rcopy(
                    xg.at[t, my_rows], xg.at[t, my_rows], b_s.at[i, t, b], b_r.at[i, t, k], bdev(b)
                ).wait_send()

    each(nc - 1, drain_z)
    rcopy(vs.at[me], vr.at[s, me], vc_s.at[me], vc_r.at[me], cdev).wait_send()
    for c in core:
        c.wait_send()
    for e in range(1, nb):
        b = lax.rem(k + e, nb)
        rcopy(
            xg2.at[me, my_rows], xg2.at[me, my_rows], b_s.at[1, me, b], b_r.at[1, me, k], bdev(b)
        ).wait_send()
        for i in range(2):
            rcopy(
                rs_send.at[i, e - 1], rs_recv.at[i, e - 1], rs_s.at[i, e - 1], rs_r.at[i, e - 1], bdev(b)
            ).wait_send()
        rcopy(
            pot.at[my_rows, my_cols], pot.at[my_rows, my_cols], p_s.at[b], p_r.at[k], bdev(b)
        ).wait_send()
    for e in range(nb):
        t, pr = peer_rows(e)
        rcopy(pot.at[pr, my_cols], pot.at[pr, my_cols], pc_s.at[t], pc_r.at[t], cdev).wait_send()
    for idx in range(len(mates)):
        rcopy(stat, stat_r.at[idx], st_s.at[idx], st_r.at[idx], cdev).wait_send()
    pot_copy.wait()


def per_device(
    nc, nb, ns,
    density, far_cols, far_bucket, far_v, far_u, near_rows, near_cols, near_tiles,
    ag_leaf, ag_grad, ag_normal, ag_arm, ag_area,
):
    cl, panels, loads = density.shape
    rank = far_v.shape[1]
    near = near_tiles.shape[0]
    count = ag_leaf.shape[0]
    half = loads // ns
    rows = cl * panels
    ch = rows // nb
    vb = cl * rank + 16
    group = 4 if nc % 4 == 0 else nc
    scale = 1.0 / math.sqrt(nc * nb * ns)
    vm = pl.BlockSpec(memory_space=pltpu.VMEM)
    sm = pl.BlockSpec(memory_space=pltpu.SMEM)
    anyspace = pl.BlockSpec(memory_space=pl.ANY)
    dma = pltpu.SemaphoreType.DMA
    pot, sec, tor = pl.pallas_call(
        functools.partial(kernel, nc, nb, ns, cl, rank, scale),
        out_shape=(
            jax.ShapeDtypeStruct((rows, loads), BF16),
            jax.ShapeDtypeStruct((cl, 3, loads), F32),
            jax.ShapeDtypeStruct((3, loads), F32),
        ),
        in_specs=[sm] * 4 + [anyspace] * 4 + [vm, anyspace, vm, vm, vm],
        out_specs=(anyspace, vm, vm),
        scratch_shapes=[
            pltpu.VMEM((nc * cl, rank, panels), BF16),
            pltpu.VMEM((nc, vb, panels), BF16),
            pltpu.VMEM((ns, nc, vb, panels), BF16),
            pltpu.VMEM((nc, ns * cl * rank, cl * panels), BF16),
            pltpu.VMEM((ns, nc, cl, rank, panels), BF16),
            pltpu.VMEM((cl, ns * (nc // group), panels, group * rank), BF16),
            pltpu.VMEM((ns, near, panels, panels), BF16),
            pltpu.VMEM((ns, 8, LANES), F32),
            pltpu.VMEM((3, count, panels), BF16),
            pltpu.VMEM((8, count), F32),
            pltpu.VMEM((count, 8), F32),
            pltpu.VMEM((nc, rows, half), BF16),
            pltpu.VMEM((nc, rows, half), BF16),
            pltpu.VMEM((cl, ns, nc, rank, half), BF16),
            pltpu.VMEM((rows, half), F32),
            pltpu.VMEM((2, nb - 1, ch, half), F32),
            pltpu.VMEM((2, nb - 1, ch, half), F32),
            pltpu.VMEM((rows, loads), BF16),
            pltpu.VMEM((16, loads), F32),
            pltpu.VMEM((nb * ns - 1, 16, loads), F32),
            pltpu.VMEM((8, loads), F32),
            pltpu.VMEM((nc - 1, 8, loads), F32),
            dma((6,)), dma((3,)), dma((3,)),
            dma((nc,)), dma((nc,)), dma((nc,)), dma((nc,)),
            dma((2, nc)), dma((2, nc)), dma((2, nc, nb)), dma((2, nc, nb)),
            dma((2, nb - 1)), dma((2, nb - 1)),
            dma((nb,)), dma((nb,)), dma((nb,)), dma((nb,)),
            dma((nb * ns - 1,)), dma((nb * ns - 1,)),
            dma((nc - 1,)), dma((nc - 1,)),
        ],
        compiler_params=pltpu.CompilerParams(
            collective_id=0, has_side_effects=True, vmem_limit_bytes=52 * 1024 * 1024
        ),
    )(
        far_cols, far_bucket, near_rows, near_cols,
        density.reshape(rows, loads), far_v,
        far_u.reshape(nc, cl, rank, panels), near_tiles,
        ag_leaf.reshape(1, count), jnp.transpose(ag_grad, (1, 0, 2)),
        ag_normal, ag_arm, ag_area.reshape(1, count),
    )
    return pot.reshape(cl, panels, loads), sec, tor


def solution(mesh):
    placed = (
        P(("design", "cluster"), None, None),
        P(("design", "cluster", "blk", "sub")),
        P(("design", "cluster", "blk", "sub")),
        P(("design", "cluster", "blk", "sub"), None, None),
        P(("design", "cluster", "blk", "sub"), None, None),
        P(("design", "cluster", "blk", "sub")),
        P(("design", "cluster", "blk", "sub")),
        P(("design", "cluster", "blk", "sub"), None, None),
        P(("design", "cluster", "blk", "sub")),
        P(("design", "cluster", "blk", "sub"), None, None),
        P("design", ("cluster", "blk", "sub")),
        P("design", ("cluster", "blk", "sub")),
        P(("design", "cluster", "blk", "sub")),
    )
    sizes = tuple(mesh.shape[a] for a in ("cluster", "blk", "sub"))
    return jax.shard_map(
        functools.partial(per_device, *sizes),
        mesh=mesh,
        in_specs=placed,
        out_specs=(
            P(("design", "cluster"), None, None),
            P(("design", "cluster"), None, None),
            P("design", None),
        ),
        check_vma=False,
    )
```

```python
import functools
import math

import jax
import jax.numpy as jnp
from jax import lax
from jax.experimental import pallas as pl
from jax.experimental.pallas import tpu as pltpu
from jax.sharding import PartitionSpec as P

F32 = jnp.float32
BF16 = jnp.bfloat16
LANES = 128


def each(count, body):
    if count <= 4:
        for i in range(count):
            body(i)
    else:
        pl.loop(0, count)(body)


def kernel(
    nc, nb, ns, cl, rank, scale,
    cols_h, bucket_h, nrow_h, ncol_h,
    dens, far_v, far_u, tiles, leaf_h, grad, normal_h, arm_h, area_h,
    pot_out, sec_out, tor_out,
    vin, vs, vr, vx, u_all, ut, nt, meta, g_v, agrow, agcol, xg1, xg2, cf, part, rs_send, rs_recv,
    pot, stat, stat_r, tor_s, tor_r,
    cols_s, bucket_s, nrow_s, ncol_s, leaf, normal, arm, area,
    loc_sem, core_s, core_r, v_s, v_r, vc_s, vc_r,
    z_s, z_r, b_s, b_r, rs_s, rs_r, p_s, p_r, pc_s, pc_r, st_s, st_r, t_s, t_r,
):
    me = lax.axis_index("cluster")
    k = lax.axis_index("blk")
    s = lax.axis_index("sub")
    rows, loads = dens.shape
    panels = rows // cl
    half = loads // ns
    ch = rows // nb
    near = tiles.shape[0]
    vrows = cl * rank
    my_rows = pl.ds(pl.multiple_of(k * ch, ch), ch)
    my_cols = pl.ds(pl.multiple_of(s * half, half), half)
    other = 1 - s

    def rcopy(src, dst, ss, rs, dev):
        return pltpu.make_async_remote_copy(
            src_ref=src, dst_ref=dst, send_sem=ss, recv_sem=rs, device_id=dev,
            device_id_type=pl.DeviceIdType.MESH,
        )

    def zdev(t):
        return {"cluster": t}

    def bdev(t):
        return {"blk": t}

    cdev = {"sub": other}

    small = [
        pltpu.make_async_copy(a, b, loc_sem.at[6 + i])
        for i, (a, b) in enumerate(
            (
                (bucket_h, bucket_s), (cols_h, cols_s), (nrow_h, nrow_s), (ncol_h, ncol_s),
                (leaf_h, leaf), (normal_h, normal), (arm_h, arm), (area_h, area),
            )
        )
    ]
    for c in small[:4]:
        c.start()
    local = [
        pltpu.make_async_copy(far_v, vin, loc_sem.at[0]),
        pltpu.make_async_copy(dens.at[:, my_cols], xg1.at[me], loc_sem.at[1]),
        pltpu.make_async_copy(far_u, u_all.at[s], loc_sem.at[2]),
        pltpu.make_async_copy(tiles, nt.at[s], loc_sem.at[3]),
        pltpu.make_async_copy(grad, g_v, loc_sem.at[4]),
    ]
    for c in local + small[4:]:
        c.start()

    bar = pltpu.get_barrier_semaphore()

    def greet_z(d):
        pl.semaphore_signal(
            bar, inc=1, device_id=zdev(lax.rem(me + d + 1, nc)), device_id_type=pl.DeviceIdType.MESH
        )

    each(nc - 1, greet_z)
    mates = [(e, g) for e in range(nb) for g in range(ns) if (e, g) != (0, 0)]
    for e, g in mates:
        pl.semaphore_signal(
            bar, inc=1,
            device_id={"blk": lax.rem(k + e, nb), "sub": lax.rem(s + g, ns)},
            device_id_type=pl.DeviceIdType.MESH,
        )

    for c in small[:4]:
        c.wait()
    rid = lax.broadcasted_iota(jnp.int32, (8, LANES), 0)
    m = jnp.zeros((8, LANES), jnp.int32)
    for i in range(near):
        m = jnp.where(rid == i, ncol_s[i], m)
        m = jnp.where(rid == near + i, nrow_s[i], m)
    meta[pl.ds(s, 1)] = m.astype(F32)[None]

    local[0].wait()
    rr = lax.broadcasted_iota(jnp.int32, (rank, panels), 0)
    hr = lax.broadcasted_iota(jnp.int32, (16, panels), 0)

    def build(a):
        head = jnp.zeros((16, panels), jnp.int32)
        for q in range(cl):
            b = bucket_s[a * cl + q]
            width = jnp.where(b > 0, lax.shift_right_logical(jnp.int32(rank), 4 - b), 0)
            blk = vin[a * cl + q]
            vs[a, q * rank : (q + 1) * rank, :] = jnp.where(
                rr < width, blk.astype(F32), 0.0
            ).astype(BF16)
            head = jnp.where(hr == q, cols_s[a * cl + q], head)
        vs[a, vrows : vrows + 16, :] = head.astype(F32).astype(BF16)

    each(nc, build)

    pl.semaphore_wait(bar, nc - 1 + len(mates))

    def send_x1(d):
        t = lax.rem(me + d + 1, nc)
        rcopy(
            dens.at[my_rows, my_cols], xg1.at[me, my_rows], z_s.at[0, t], z_r.at[0, me], zdev(t)
        ).start()

    each(nc - 1, send_x1)

    def send_v(d):
        t = lax.rem(me + d + 1, nc)
        rcopy(vs.at[t], vr.at[s, me], v_s.at[t], v_r.at[me], zdev(t)).start()

    each(nc - 1, send_v)
    core = [
        rcopy(far_u, u_all.at[s], core_s.at[0], core_r.at[0], cdev),
        rcopy(tiles, nt.at[s], core_s.at[1], core_r.at[1], cdev),
        rcopy(meta.at[s], meta.at[s], core_s.at[2], core_r.at[2], cdev),
    ]
    for c in core:
        c.start()
    rcopy(vs.at[me], vr.at[s, me], vc_s.at[me], vc_r.at[me], cdev).start()

    for c in small[4:]:
        c.wait()
    agrow[0:3, :] = normal[...]
    agrow[3:6, :] = arm[...]
    agrow[6:7, :] = area[...]
    agrow[7:8, :] = leaf[...].astype(F32)
    agcol[...] = jnp.transpose(agrow[...])

    def forward_x(i, xg):
        def body(d):
            c = lax.rem(me + nc - d - 1, nc)
            rcopy(
                xg.at[c, my_rows], xg.at[c, my_rows], z_s.at[i, c], z_r.at[i, c], zdev(c)
            ).wait_recv()
            share(i, xg, c)

        each(nc - 1, body)

    def share(i, xg, c):
        for e in range(1, nb):
            t = lax.rem(k + e, nb)
            rcopy(
                xg.at[c, my_rows], xg.at[c, my_rows], b_s.at[i, c, t], b_r.at[i, c, k], bdev(t)
            ).start()

    def peer_rows(e):
        t = lax.rem(k + nb - e, nb)
        return t, pl.ds(pl.multiple_of(t * ch, ch), ch)

    def wait_shared(i, xg, c):
        for e in range(1, nb):
            t, pr = peer_rows(e)
            rcopy(
                xg.at[c, pr], xg.at[c, pr], b_s.at[i, c, t], b_r.at[i, c, t], bdev(t)
            ).wait_recv()

    forward_x(0, xg1)

    def forward_v(d):
        c = lax.rem(me + nc - d - 1, nc)
        rcopy(vs.at[c], vr.at[s, c], v_s.at[c], v_r.at[c], zdev(c)).wait_recv()
        rcopy(vr.at[s, c], vr.at[s, c], vc_s.at[c], vc_r.at[c], cdev).start()

    each(nc - 1, forward_v)

    local[2].wait()
    core[0].wait_recv()
    group = 4 if nc % 4 == 0 else nc

    for q in range(cl):
        for sp in range(ns):
            def turn(i, q=q, sp=sp):
                u = u_all[sp, pl.ds(i * group, group), q].reshape(group * rank, panels)
                ut[q, sp * (nc // group) + i] = jnp.transpose(u)

            each(nc // group, turn)

    vr[pl.ds(s, 1), pl.ds(me, 1)] = vs[pl.ds(me, 1)][None]

    def expand(d):
        c = lax.rem(me + nc - d, nc)
        rcopy(vs.at[c], vr.at[other, c], vc_s.at[c], vc_r.at[c], cdev).wait_recv()
        for sp in range(ns):
            for q in range(cl):
                v = vr[sp, c, q * rank : (q + 1) * rank, :]
                h = vr[sp, c, vrows : vrows + 16, :][q : q + 1]
                r0 = (sp * cl + q) * rank
                for j in range(cl):
                    w = jnp.where(h.astype(F32) == float(j), 1.0, 0.0).astype(BF16)
                    vx[c, r0 : r0 + rank, j * panels : (j + 1) * panels] = v * w

    each(nc, expand)

    local[1].wait()
    local[3].wait()
    core[1].wait_recv()
    core[2].wait_recv()

    def apply(i, xg):
        def coeff(d):
            c = lax.rem(me + nc - d, nc)
            if i == 0:
                if isinstance(d, int):
                    if d > 0:
                        wait_shared(i, xg, c)
                else:
                    pl.when(d > 0)(lambda: wait_shared(i, xg, c))
            else:
                wait_shared(i, xg, c)
            y = jnp.dot(vx[c], xg[c], preferred_element_type=F32).astype(BF16)
            for sp in range(ns):
                for q in range(cl):
                    r0 = (sp * cl + q) * rank
                    cf[q, sp, c] = y[r0 : r0 + rank]

        each(nc, coeff)
        acc = []
        for q in range(cl):
            total = jnp.zeros((panels, half), F32)
            for sp in range(ns):
                def far_step(gi, total, q=q, sp=sp):
                    w = cf[q, sp, pl.ds(gi * group, group)].reshape(group * rank, half)
                    return total + jnp.dot(
                        ut[q, sp * (nc // group) + gi], w, preferred_element_type=F32
                    )

                if nc == group:
                    total = far_step(0, total)
                else:
                    total = lax.fori_loop(0, nc // group, far_step, total)
            acc.append(total)
        for sp in range(ns):
            for n in range(near):
                col = meta[sp, n : n + 1, :]
                row = meta[sp, near + n : near + n + 1, :]
                chosen = jnp.zeros((panels, half), BF16)
                for j in range(3 * cl):
                    c = lax.rem(me + nc - 1 + j // cl, nc)
                    w = jnp.where(col == float(j), 1.0, 0.0).astype(BF16)
                    p0 = (j % cl) * panels
                    chosen = chosen + xg[c, p0 : p0 + panels, :] * w
                val = jnp.dot(nt[sp, n], chosen, preferred_element_type=F32)
                for q in range(cl):
                    acc[q] = acc[q] + jnp.where(row == float(q), val, 0.0)
        for q in range(cl):
            part[q * panels : (q + 1) * panels, :] = acc[q]
        for e in range(1, nb):
            t = lax.rem(k + e, nb)
            tr = pl.ds(pl.multiple_of(t * ch, ch), ch)
            rs_send[i, e - 1] = part[tr, :].astype(rs_send.dtype)
            rcopy(
                rs_send.at[i, e - 1], rs_recv.at[i, e - 1], rs_s.at[i, e - 1], rs_r.at[i, e - 1], bdev(t)
            ).start()
        out = part[my_rows, :]
        for e in range(1, nb):
            rcopy(
                rs_send.at[i, e - 1], rs_recv.at[i, e - 1], rs_s.at[i, e - 1], rs_r.at[i, e - 1], bdev(k)
            ).wait_recv()
            out = out + rs_recv[i, e - 1].astype(F32)
        return (0.5 * xg[me, my_rows, :].astype(F32) + out).astype(BF16)

    first = apply(0, xg1)
    xg2[me, my_rows, :] = first

    def send_x2(d):
        t = lax.rem(me + d + 1, nc)
        rcopy(
            xg2.at[me, my_rows], xg2.at[me, my_rows], z_s.at[1, t], z_r.at[1, me], zdev(t)
        ).start()

    each(nc - 1, send_x2)
    share(1, xg2, me)
    forward_x(1, xg2)
    potential = apply(1, xg2)

    pot[my_rows, my_cols] = potential
    for e in range(1, nb):
        t = lax.rem(k + e, nb)
        rcopy(
            pot.at[my_rows, my_cols], pot.at[my_rows, my_cols], p_s.at[t], p_r.at[k], bdev(t)
        ).start()
    rcopy(pot.at[my_rows, my_cols], pot.at[my_rows, my_cols], pc_s.at[k], pc_r.at[k], cdev).start()
    for e in range(1, nb):
        t, pr = peer_rows(e)
        rcopy(
            pot.at[pr, my_cols], pot.at[pr, my_cols], p_s.at[t], p_r.at[t], bdev(t)
        ).wait_recv()
        rcopy(pot.at[pr, my_cols], pot.at[pr, my_cols], pc_s.at[t], pc_r.at[t], cdev).start()
    oc = pl.ds(pl.multiple_of(other * half, half), half)
    for e in range(nb):
        t, pr = peer_rows(e)
        rcopy(pot.at[pr, oc], pot.at[pr, oc], pc_s.at[t], pc_r.at[t], cdev).wait_recv()
    pot_copy = pltpu.make_async_copy(pot, pot_out, loc_sem.at[5])
    pot_copy.start()

    local[4].wait()
    count = g_v.shape[1]
    step = 64

    def stress(gi, acc):
        g0 = pl.multiple_of(gi * step, step)
        cols = agcol[pl.ds(g0, step), :]
        n = [cols[:, j : j + 1] for j in range(3)]
        a = [cols[:, 3 + j : 4 + j] for j in range(3)]
        ar = cols[:, 6:7]
        lf = cols[:, 7:8]
        field = []
        for j in range(3):
            g = g_v[j, pl.ds(g0, step), :]
            fj = jnp.zeros((step, loads), F32)
            for q in range(cl):
                v = jnp.dot(g, pot[q * panels : (q + 1) * panels, :], preferred_element_type=F32)
                fj = jnp.where(lf == float(q), v, fj)
            field.append(fj)
        along = field[0] * n[0] + field[1] * n[1] + field[2] * n[2]
        sq = 0.5 * (field[0] * field[0] + field[1] * field[1] + field[2] * field[2])
        w = [(along * field[j] - sq * n[j]) * ar for j in range(3)]
        terms = []
        for q in range(cl):
            for j in range(3):
                terms.append(jnp.where(lf == float(q), w[j], 0.0))
        for j in range(3):
            x, y = (j + 1) % 3, (j + 2) % 3
            terms.append(a[x] * w[y] - a[y] * w[x])
        return tuple(
            o + jnp.sum(t.reshape(step // 8, 8, loads), axis=0) for o, t in zip(acc, terms)
        )

    nst = cl * 3 + 3
    zero = tuple(jnp.zeros((8, loads), F32) for _ in range(nst))
    sums = lax.fori_loop(0, count // step, stress, zero)
    for i in range(nst):
        stat[i : i + 1, :] = jnp.sum(sums[i], axis=0, keepdims=True)
    for idx, (e, g) in enumerate(mates):
        rcopy(
            stat, stat_r.at[idx], st_s.at[idx], st_r.at[idx],
            {"blk": lax.rem(k + e, nb), "sub": lax.rem(s + g, ns)},
        ).start()
    tot = stat[0:nst, :]
    for idx in range(len(mates)):
        rcopy(stat, stat_r.at[idx], st_s.at[idx], st_r.at[idx], cdev).wait_recv()
        tot = tot + stat_r[idx, 0:nst, :]
    tor_s[0:3, :] = tot[cl * 3 : cl * 3 + 3]

    def send_t(d):
        t = lax.rem(me + d + 1, nc)
        rcopy(tor_s, tor_r.at[d], t_s.at[d], t_r.at[d], zdev(t)).start()

    each(nc - 1, send_t)
    for q in range(cl):
        sec_out[q] = tot[q * 3 : q * 3 + 3]

    def wait_t(d):
        rcopy(tor_s, tor_r.at[d], t_s.at[d], t_r.at[d], zdev(me)).wait_recv()

    each(nc - 1, wait_t)
    if nc - 1 <= 4:
        tt = tor_s[0:3, :]
        for d in range(nc - 1):
            tt = tt + tor_r[d, 0:3, :]
    else:
        tt = lax.fori_loop(0, nc - 1, lambda d, t: t + tor_r[d, 0:3, :], tor_s[0:3, :])
    tor_out[...] = tt * scale

    def drain_z(d):
        t = lax.rem(me + d + 1, nc)
        rcopy(
            dens.at[my_rows, my_cols], xg1.at[me, my_rows], z_s.at[0, t], z_r.at[0, me], zdev(t)
        ).wait_send()
        rcopy(vs.at[t], vr.at[s, me], v_s.at[t], v_r.at[me], zdev(t)).wait_send()
        rcopy(
            xg2.at[me, my_rows], xg2.at[me, my_rows], z_s.at[1, t], z_r.at[1, me], zdev(t)
        ).wait_send()
        rcopy(tor_s, tor_r.at[d], t_s.at[d], t_r.at[d], zdev(t)).wait_send()
        rcopy(vr.at[s, t], vr.at[s, t], vc_s.at[t], vc_r.at[t], cdev).wait_send()
        for e in range(1, nb):
            b = lax.rem(k + e, nb)
            for i, xg in ((0, xg1), (1, xg2)):
                rcopy(
                    xg.at[t, my_rows], xg.at[t, my_rows], b_s.at[i, t, b], b_r.at[i, t, k], bdev(b)
                ).wait_send()

    each(nc - 1, drain_z)
    rcopy(vs.at[me], vr.at[s, me], vc_s.at[me], vc_r.at[me], cdev).wait_send()
    for c in core:
        c.wait_send()
    for e in range(1, nb):
        b = lax.rem(k + e, nb)
        rcopy(
            xg2.at[me, my_rows], xg2.at[me, my_rows], b_s.at[1, me, b], b_r.at[1, me, k], bdev(b)
        ).wait_send()
        for i in range(2):
            rcopy(
                rs_send.at[i, e - 1], rs_recv.at[i, e - 1], rs_s.at[i, e - 1], rs_r.at[i, e - 1], bdev(b)
            ).wait_send()
        rcopy(
            pot.at[my_rows, my_cols], pot.at[my_rows, my_cols], p_s.at[b], p_r.at[k], bdev(b)
        ).wait_send()
    for e in range(nb):
        t, pr = peer_rows(e)
        rcopy(pot.at[pr, my_cols], pot.at[pr, my_cols], pc_s.at[t], pc_r.at[t], cdev).wait_send()
    for idx in range(len(mates)):
        rcopy(stat, stat_r.at[idx], st_s.at[idx], st_r.at[idx], cdev).wait_send()
    pot_copy.wait()


def per_device(
    nc, nb, ns,
    density, far_cols, far_bucket, far_v, far_u, near_rows, near_cols, near_tiles,
    ag_leaf, ag_grad, ag_normal, ag_arm, ag_area,
):
    cl, panels, loads = density.shape
    rank = far_v.shape[1]
    near = near_tiles.shape[0]
    count = ag_leaf.shape[0]
    half = loads // ns
    rows = cl * panels
    ch = rows // nb
    vb = cl * rank + 16
    group = 4 if nc % 4 == 0 else nc
    scale = 1.0 / math.sqrt(nc * nb * ns)
    vm = pl.BlockSpec(memory_space=pltpu.VMEM)
    anyspace = pl.BlockSpec(memory_space=pl.ANY)
    dma = pltpu.SemaphoreType.DMA
    pot, sec, tor = pl.pallas_call(
        functools.partial(kernel, nc, nb, ns, cl, rank, scale),
        out_shape=(
            jax.ShapeDtypeStruct((rows, loads), BF16),
            jax.ShapeDtypeStruct((cl, 3, loads), F32),
            jax.ShapeDtypeStruct((3, loads), F32),
        ),
        in_specs=[anyspace] * 13,
        out_specs=(anyspace, vm, vm),
        scratch_shapes=[
            pltpu.VMEM((nc * cl, rank, panels), BF16),
            pltpu.VMEM((nc, vb, panels), BF16),
            pltpu.VMEM((ns, nc, vb, panels), BF16),
            pltpu.VMEM((nc, ns * cl * rank, cl * panels), BF16),
            pltpu.VMEM((ns, nc, cl, rank, panels), BF16),
            pltpu.VMEM((cl, ns * (nc // group), panels, group * rank), BF16),
            pltpu.VMEM((ns, near, panels, panels), BF16),
            pltpu.VMEM((ns, 8, LANES), F32),
            pltpu.VMEM((3, count, panels), BF16),
            pltpu.VMEM((8, count), F32),
            pltpu.VMEM((count, 8), F32),
            pltpu.VMEM((nc, rows, half), BF16),
            pltpu.VMEM((nc, rows, half), BF16),
            pltpu.VMEM((cl, ns, nc, rank, half), BF16),
            pltpu.VMEM((rows, half), F32),
            pltpu.VMEM((2, nb - 1, ch, half), BF16),
            pltpu.VMEM((2, nb - 1, ch, half), BF16),
            pltpu.VMEM((rows, loads), BF16),
            pltpu.VMEM((16, loads), F32),
            pltpu.VMEM((nb * ns - 1, 16, loads), F32),
            pltpu.VMEM((8, loads), F32),
            pltpu.VMEM((nc - 1, 8, loads), F32),
            pltpu.SMEM((nc * cl,), jnp.int32),
            pltpu.SMEM((nc * cl,), jnp.int32),
            pltpu.SMEM((near,), jnp.int32),
            pltpu.SMEM((near,), jnp.int32),
            pltpu.VMEM((1, count), jnp.int32),
            pltpu.VMEM((3, count), F32),
            pltpu.VMEM((3, count), F32),
            pltpu.VMEM((1, count), F32),
            dma((14,)), dma((3,)), dma((3,)),
            dma((nc,)), dma((nc,)), dma((nc,)), dma((nc,)),
            dma((2, nc)), dma((2, nc)), dma((2, nc, nb)), dma((2, nc, nb)),
            dma((2, nb - 1)), dma((2, nb - 1)),
            dma((nb,)), dma((nb,)), dma((nb,)), dma((nb,)),
            dma((nb * ns - 1,)), dma((nb * ns - 1,)),
            dma((nc - 1,)), dma((nc - 1,)),
        ],
        compiler_params=pltpu.CompilerParams(
            collective_id=0, has_side_effects=True, vmem_limit_bytes=63 * 1024 * 1024
        ),
    )(
        far_cols, far_bucket, near_rows, near_cols,
        density.reshape(rows, loads), far_v,
        far_u.reshape(nc, cl, rank, panels), near_tiles,
        ag_leaf.reshape(1, count), jnp.transpose(ag_grad, (1, 0, 2)),
        ag_normal, ag_arm, ag_area.reshape(1, count),
    )
    return pot.reshape(cl, panels, loads), sec, tor


def solution(mesh):
    placed = (
        P(("design", "cluster"), None, None),
        P(("design", "cluster", "blk", "sub")),
        P(("design", "cluster", "blk", "sub")),
        P(("design", "cluster", "blk", "sub"), None, None),
        P(("design", "cluster", "blk", "sub"), None, None),
        P(("design", "cluster", "blk", "sub")),
        P(("design", "cluster", "blk", "sub")),
        P(("design", "cluster", "blk", "sub"), None, None),
        P(("design", "cluster", "blk", "sub")),
        P(("design", "cluster", "blk", "sub"), None, None),
        P("design", ("cluster", "blk", "sub")),
        P("design", ("cluster", "blk", "sub")),
        P(("design", "cluster", "blk", "sub")),
    )
    sizes = tuple(mesh.shape[a] for a in ("cluster", "blk", "sub"))
    return jax.shard_map(
        functools.partial(per_device, *sizes),
        mesh=mesh,
        in_specs=placed,
        out_specs=(
            P(("design", "cluster"), None, None),
            P(("design", "cluster"), None, None),
            P("design", None),
        ),
        check_vma=False,
    )
```

```python
import functools
import math

import jax
import jax.numpy as jnp
from jax import lax
from jax.experimental import pallas as pl
from jax.experimental.pallas import tpu as pltpu
from jax.sharding import PartitionSpec as P

F32 = jnp.float32
BF16 = jnp.bfloat16
LANES = 128


def each(count, body):
    if count <= 4:
        for i in range(count):
            body(i)
    else:
        pl.loop(0, count)(body)


def kernel(
    nc, nb, ns, cl, rank, scale,
    cols_h, bucket_h, nrow_h, ncol_h,
    dens, far_v, far_u, tiles, leaf_h, grad, normal_h, arm_h, area_h,
    pot_out, sec_out, tor_out,
    vin, vs, vr, vx, u_all, ut, nt, meta, g_v, agrow, agcol, xg1, xg2, cf, part, rs_send, rs_recv,
    pot, stat, stat_r, tor_s, tor_r,
    cols_s, bucket_s, nrow_s, ncol_s, leaf, normal, arm, area,
    loc_sem, core_s, core_r, v_s, v_r, vc_s, vc_r,
    z_s, z_r, b_s, b_r, rs_s, rs_r, p_s, p_r, pc_s, pc_r, st_s, st_r, t_s, t_r,
):
    me = lax.axis_index("cluster")
    k = lax.axis_index("blk")
    s = lax.axis_index("sub")
    rows, loads = dens.shape
    panels = rows // cl
    half = loads // ns
    ch = rows // nb
    near = tiles.shape[0]
    vrows = cl * rank
    my_rows = pl.ds(pl.multiple_of(k * ch, ch), ch)
    my_cols = pl.ds(pl.multiple_of(s * half, half), half)
    other = 1 - s

    def rcopy(src, dst, ss, rs, dev):
        return pltpu.make_async_remote_copy(
            src_ref=src, dst_ref=dst, send_sem=ss, recv_sem=rs, device_id=dev,
            device_id_type=pl.DeviceIdType.MESH,
        )

    def zdev(t):
        return {"cluster": t}

    def bdev(t):
        return {"blk": t}

    cdev = {"sub": other}

    small = [
        pltpu.make_async_copy(a, b, loc_sem.at[6 + i])
        for i, (a, b) in enumerate(
            (
                (bucket_h, bucket_s), (cols_h, cols_s), (nrow_h, nrow_s), (ncol_h, ncol_s),
                (leaf_h, leaf), (normal_h, normal), (arm_h, arm), (area_h, area),
            )
        )
    ]
    for c in small[:4]:
        c.start()
    local = [
        pltpu.make_async_copy(far_v, vin, loc_sem.at[0]),
        pltpu.make_async_copy(dens.at[:, my_cols], xg1.at[me], loc_sem.at[1]),
        pltpu.make_async_copy(far_u, u_all.at[s], loc_sem.at[2]),
        pltpu.make_async_copy(tiles, nt.at[s], loc_sem.at[3]),
        pltpu.make_async_copy(grad, g_v, loc_sem.at[4]),
    ]
    for c in local + small[4:]:
        c.start()

    bar = pltpu.get_barrier_semaphore()

    def greet_z(d):
        pl.semaphore_signal(
            bar, inc=1, device_id=zdev(lax.rem(me + d + 1, nc)), device_id_type=pl.DeviceIdType.MESH
        )

    each(nc - 1, greet_z)
    mates = [(e, g) for e in range(nb) for g in range(ns) if (e, g) != (0, 0)]
    for e, g in mates:
        pl.semaphore_signal(
            bar, inc=1,
            device_id={"blk": lax.rem(k + e, nb), "sub": lax.rem(s + g, ns)},
            device_id_type=pl.DeviceIdType.MESH,
        )

    for c in small[:4]:
        c.wait()
    rid = lax.broadcasted_iota(jnp.int32, (8, LANES), 0)
    m = jnp.zeros((8, LANES), jnp.int32)
    for i in range(near):
        m = jnp.where(rid == i, ncol_s[i], m)
        m = jnp.where(rid == near + i, nrow_s[i], m)
    meta[pl.ds(s, 1)] = m.astype(F32)[None]

    local[0].wait()
    rr = lax.broadcasted_iota(jnp.int32, (rank, panels), 0)
    hr = lax.broadcasted_iota(jnp.int32, (16, panels), 0)

    def build(a):
        head = jnp.zeros((16, panels), jnp.int32)
        for q in range(cl):
            b = bucket_s[a * cl + q]
            width = jnp.where(b > 0, lax.shift_right_logical(jnp.int32(rank), 4 - b), 0)
            blk = vin[a * cl + q]
            vs[a, q * rank : (q + 1) * rank, :] = jnp.where(
                rr < width, blk.astype(F32), 0.0
            ).astype(BF16)
            head = jnp.where(hr == q, cols_s[a * cl + q], head)
        vs[a, vrows : vrows + 16, :] = head.astype(F32).astype(BF16)

    each(nc, build)

    pl.semaphore_wait(bar, nc - 1 + len(mates))

    def send_x1(d):
        t = lax.rem(me + d + 1, nc)
        rcopy(
            dens.at[my_rows, my_cols], xg1.at[me, my_rows], z_s.at[0, t], z_r.at[0, me], zdev(t)
        ).start()

    each(nc - 1, send_x1)

    def send_v(d):
        t = lax.rem(me + d + 1, nc)
        rcopy(vs.at[t], vr.at[s, me], v_s.at[t], v_r.at[me], zdev(t)).start()

    each(nc - 1, send_v)
    core = [
        rcopy(far_u, u_all.at[s], core_s.at[0], core_r.at[0], cdev),
        rcopy(tiles, nt.at[s], core_s.at[1], core_r.at[1], cdev),
        rcopy(meta.at[s], meta.at[s], core_s.at[2], core_r.at[2], cdev),
    ]
    for c in core:
        c.start()
    rcopy(vs.at[me], vr.at[s, me], vc_s.at[me], vc_r.at[me], cdev).start()

    for c in small[4:]:
        c.wait()
    agrow[0:3, :] = normal[...]
    agrow[3:6, :] = arm[...]
    agrow[6:7, :] = area[...]
    agrow[7:8, :] = leaf[...].astype(F32)
    agcol[...] = jnp.transpose(agrow[...])

    def forward_x(i, xg):
        def body(d):
            c = lax.rem(me + nc - d - 1, nc)
            rcopy(
                xg.at[c, my_rows], xg.at[c, my_rows], z_s.at[i, c], z_r.at[i, c], zdev(c)
            ).wait_recv()
            share(i, xg, c)

        each(nc - 1, body)

    def share(i, xg, c):
        for e in range(1, nb):
            t = lax.rem(k + e, nb)
            rcopy(
                xg.at[c, my_rows], xg.at[c, my_rows], b_s.at[i, c, t], b_r.at[i, c, k], bdev(t)
            ).start()

    def peer_rows(e):
        t = lax.rem(k + nb - e, nb)
        return t, pl.ds(pl.multiple_of(t * ch, ch), ch)

    def wait_shared(i, xg, c):
        for e in range(1, nb):
            t, pr = peer_rows(e)
            rcopy(
                xg.at[c, pr], xg.at[c, pr], b_s.at[i, c, t], b_r.at[i, c, t], bdev(t)
            ).wait_recv()

    forward_x(0, xg1)

    def forward_v(d):
        c = lax.rem(me + nc - d - 1, nc)
        rcopy(vs.at[c], vr.at[s, c], v_s.at[c], v_r.at[c], zdev(c)).wait_recv()
        rcopy(vr.at[s, c], vr.at[s, c], vc_s.at[c], vc_r.at[c], cdev).start()

    each(nc - 1, forward_v)

    local[2].wait()
    core[0].wait_recv()
    group = 4 if nc % 4 == 0 else nc

    for q in range(cl):
        for sp in range(ns):
            def turn(i, q=q, sp=sp):
                u = u_all[sp, pl.ds(i * group, group), q].reshape(group * rank, panels)
                ut[q, sp * (nc // group) + i] = jnp.transpose(u)

            each(nc // group, turn)

    vr[pl.ds(s, 1), pl.ds(me, 1)] = vs[pl.ds(me, 1)][None]

    def expand(d):
        c = lax.rem(me + nc - d, nc)
        rcopy(vs.at[c], vr.at[other, c], vc_s.at[c], vc_r.at[c], cdev).wait_recv()
        for sp in range(ns):
            for q in range(cl):
                v = vr[sp, c, q * rank : (q + 1) * rank, :]
                h = vr[sp, c, vrows : vrows + 16, :][q : q + 1]
                r0 = (sp * cl + q) * rank
                for j in range(cl):
                    w = jnp.where(h.astype(F32) == float(j), 1.0, 0.0).astype(BF16)
                    vx[c, r0 : r0 + rank, j * panels : (j + 1) * panels] = v * w

    each(nc, expand)

    local[1].wait()
    local[3].wait()
    core[1].wait_recv()
    core[2].wait_recv()

    def apply(i, xg):
        def coeff(d):
            c = lax.rem(me + nc - d, nc)
            if i == 0:
                if isinstance(d, int):
                    if d > 0:
                        wait_shared(i, xg, c)
                else:
                    pl.when(d > 0)(lambda: wait_shared(i, xg, c))
            else:
                wait_shared(i, xg, c)
            y = jnp.dot(vx[c], xg[c], preferred_element_type=F32).astype(BF16)
            for sp in range(ns):
                for q in range(cl):
                    r0 = (sp * cl + q) * rank
                    cf[q, sp, c] = y[r0 : r0 + rank]

        each(nc, coeff)
        acc = []
        for q in range(cl):
            total = jnp.zeros((panels, half), F32)
            for sp in range(ns):
                def far_step(gi, total, q=q, sp=sp):
                    w = cf[q, sp, pl.ds(gi * group, group)].reshape(group * rank, half)
                    return total + jnp.dot(
                        ut[q, sp * (nc // group) + gi], w, preferred_element_type=F32
                    )

                if nc == group:
                    total = far_step(0, total)
                else:
                    total = lax.fori_loop(0, nc // group, far_step, total)
            acc.append(total)
        for sp in range(ns):
            for n in range(near):
                col = meta[sp, n : n + 1, :]
                row = meta[sp, near + n : near + n + 1, :]
                chosen = jnp.zeros((panels, half), BF16)
                for j in range(3 * cl):
                    c = lax.rem(me + nc - 1 + j // cl, nc)
                    w = jnp.where(col == float(j), 1.0, 0.0).astype(BF16)
                    p0 = (j % cl) * panels
                    chosen = chosen + xg[c, p0 : p0 + panels, :] * w
                val = jnp.dot(nt[sp, n], chosen, preferred_element_type=F32)
                for q in range(cl):
                    acc[q] = acc[q] + jnp.where(row == float(q), val, 0.0)
        for q in range(cl):
            part[q * panels : (q + 1) * panels, :] = acc[q]
        for e in range(1, nb):
            t = lax.rem(k + e, nb)
            tr = pl.ds(pl.multiple_of(t * ch, ch), ch)
            rs_send[i, e - 1] = part[tr, :].astype(rs_send.dtype)
            rcopy(
                rs_send.at[i, e - 1], rs_recv.at[i, e - 1], rs_s.at[i, e - 1], rs_r.at[i, e - 1], bdev(t)
            ).start()
        out = part[my_rows, :]
        for e in range(1, nb):
            rcopy(
                rs_send.at[i, e - 1], rs_recv.at[i, e - 1], rs_s.at[i, e - 1], rs_r.at[i, e - 1], bdev(k)
            ).wait_recv()
            out = out + rs_recv[i, e - 1].astype(F32)
        return (0.5 * xg[me, my_rows, :].astype(F32) + out).astype(BF16)

    first = apply(0, xg1)
    xg2[me, my_rows, :] = first

    def send_x2(d):
        t = lax.rem(me + d + 1, nc)
        rcopy(
            xg2.at[me, my_rows], xg2.at[me, my_rows], z_s.at[1, t], z_r.at[1, me], zdev(t)
        ).start()

    each(nc - 1, send_x2)
    share(1, xg2, me)
    forward_x(1, xg2)
    potential = apply(1, xg2)

    pot[my_rows, my_cols] = potential
    for e in range(1, nb):
        t = lax.rem(k + e, nb)
        rcopy(
            pot.at[my_rows, my_cols], pot.at[my_rows, my_cols], p_s.at[t], p_r.at[k], bdev(t)
        ).start()
    rcopy(pot.at[my_rows, my_cols], pot.at[my_rows, my_cols], pc_s.at[k], pc_r.at[k], cdev).start()
    for e in range(1, nb):
        t, pr = peer_rows(e)
        rcopy(
            pot.at[pr, my_cols], pot.at[pr, my_cols], p_s.at[t], p_r.at[t], bdev(t)
        ).wait_recv()
        rcopy(pot.at[pr, my_cols], pot.at[pr, my_cols], pc_s.at[t], pc_r.at[t], cdev).start()
    oc = pl.ds(pl.multiple_of(other * half, half), half)
    for e in range(nb):
        t, pr = peer_rows(e)
        rcopy(pot.at[pr, oc], pot.at[pr, oc], pc_s.at[t], pc_r.at[t], cdev).wait_recv()
    pot_copy = pltpu.make_async_copy(pot, pot_out, loc_sem.at[5])
    pot_copy.start()

    local[4].wait()
    count = g_v.shape[1]
    step = 64

    def stress(gi, acc):
        g0 = pl.multiple_of(gi * step, step)
        cols = agcol[pl.ds(g0, step), :]
        n = [cols[:, j : j + 1] for j in range(3)]
        a = [cols[:, 3 + j : 4 + j] for j in range(3)]
        ar = cols[:, 6:7]
        lf = cols[:, 7:8]
        field = []
        for j in range(3):
            g = g_v[j, pl.ds(g0, step), :]
            fj = jnp.zeros((step, loads), F32)
            for q in range(cl):
                v = jnp.dot(g, pot[q * panels : (q + 1) * panels, :], preferred_element_type=F32)
                fj = jnp.where(lf == float(q), v, fj)
            field.append(fj)
        along = field[0] * n[0] + field[1] * n[1] + field[2] * n[2]
        sq = 0.5 * (field[0] * field[0] + field[1] * field[1] + field[2] * field[2])
        w = [(along * field[j] - sq * n[j]) * ar for j in range(3)]
        terms = []
        for q in range(cl):
            for j in range(3):
                terms.append(jnp.where(lf == float(q), w[j], 0.0))
        for j in range(3):
            x, y = (j + 1) % 3, (j + 2) % 3
            terms.append(a[x] * w[y] - a[y] * w[x])
        return tuple(
            o + jnp.sum(t.reshape(step // 8, 8, loads), axis=0) for o, t in zip(acc, terms)
        )

    nst = cl * 3 + 3
    zero = tuple(jnp.zeros((8, loads), F32) for _ in range(nst))
    sums = lax.fori_loop(0, count // step, stress, zero)
    for i in range(nst):
        stat[i : i + 1, :] = jnp.sum(sums[i], axis=0, keepdims=True)
    for idx, (e, g) in enumerate(mates):
        rcopy(
            stat, stat_r.at[idx], st_s.at[idx], st_r.at[idx],
            {"blk": lax.rem(k + e, nb), "sub": lax.rem(s + g, ns)},
        ).start()
    tot = stat[0:nst, :]
    for idx in range(len(mates)):
        rcopy(stat, stat_r.at[idx], st_s.at[idx], st_r.at[idx], cdev).wait_recv()
        tot = tot + stat_r[idx, 0:nst, :]
    tor_s[0:3, :] = tot[cl * 3 : cl * 3 + 3]

    def send_t(d):
        t = lax.rem(me + d + 1, nc)
        rcopy(tor_s, tor_r.at[d], t_s.at[d], t_r.at[d], zdev(t)).start()

    each(nc - 1, send_t)
    for q in range(cl):
        sec_out[q] = tot[q * 3 : q * 3 + 3]

    def wait_t(d):
        rcopy(tor_s, tor_r.at[d], t_s.at[d], t_r.at[d], zdev(me)).wait_recv()

    each(nc - 1, wait_t)
    if nc - 1 <= 4:
        tt = tor_s[0:3, :]
        for d in range(nc - 1):
            tt = tt + tor_r[d, 0:3, :]
    else:
        tt = lax.fori_loop(0, nc - 1, lambda d, t: t + tor_r[d, 0:3, :], tor_s[0:3, :])
    tor_out[...] = tt * scale

    def drain_z(d):
        t = lax.rem(me + d + 1, nc)
        rcopy(
            dens.at[my_rows, my_cols], xg1.at[me, my_rows], z_s.at[0, t], z_r.at[0, me], zdev(t)
        ).wait_send()
        rcopy(vs.at[t], vr.at[s, me], v_s.at[t], v_r.at[me], zdev(t)).wait_send()
        rcopy(
            xg2.at[me, my_rows], xg2.at[me, my_rows], z_s.at[1, t], z_r.at[1, me], zdev(t)
        ).wait_send()
        rcopy(tor_s, tor_r.at[d], t_s.at[d], t_r.at[d], zdev(t)).wait_send()
        rcopy(vr.at[s, t], vr.at[s, t], vc_s.at[t], vc_r.at[t], cdev).wait_send()
        for e in range(1, nb):
            b = lax.rem(k + e, nb)
            for i, xg in ((0, xg1), (1, xg2)):
                rcopy(
                    xg.at[t, my_rows], xg.at[t, my_rows], b_s.at[i, t, b], b_r.at[i, t, k], bdev(b)
                ).wait_send()

    each(nc - 1, drain_z)
    rcopy(vs.at[me], vr.at[s, me], vc_s.at[me], vc_r.at[me], cdev).wait_send()
    for c in core:
        c.wait_send()
    for e in range(1, nb):
        b = lax.rem(k + e, nb)
        rcopy(
            xg2.at[me, my_rows], xg2.at[me, my_rows], b_s.at[1, me, b], b_r.at[1, me, k], bdev(b)
        ).wait_send()
        for i in range(2):
            rcopy(
                rs_send.at[i, e - 1], rs_recv.at[i, e - 1], rs_s.at[i, e - 1], rs_r.at[i, e - 1], bdev(b)
            ).wait_send()
        rcopy(
            pot.at[my_rows, my_cols], pot.at[my_rows, my_cols], p_s.at[b], p_r.at[k], bdev(b)
        ).wait_send()
    for e in range(nb):
        t, pr = peer_rows(e)
        rcopy(pot.at[pr, my_cols], pot.at[pr, my_cols], pc_s.at[t], pc_r.at[t], cdev).wait_send()
    for idx in range(len(mates)):
        rcopy(stat, stat_r.at[idx], st_s.at[idx], st_r.at[idx], cdev).wait_send()
    pot_copy.wait()


def kernel4(
    nc, nb, ns, cl, rank, scale,
    cols_h, bucket_h, nrow_h, ncol_h,
    dens, far_v, far_u, tiles, leaf_h, grad, normal_h, arm_h, area_h,
    pot_out, sec_out, tor_out,
    vin, vs, vr, u_all, ut, nt, meta, g_v, agrow, agcol, dv, xg1, xg2, cf, pk,
    pot, stat, stat_r, tor_s, tor_r,
    cols_s, bucket_s, nrow_s, ncol_s, leaf, normal, arm, area,
    loc_sem, wx_s, wx_r, wc_s, wc_r, v_s, v_r, vx_s, vx_r, vc_s, vc_r,
    z_s, z_r, p_s, p_r, st_s, st_r, t_s, t_r,
):
    me = lax.axis_index("cluster")
    k = lax.axis_index("blk")
    s = lax.axis_index("sub")
    w = k * ns + s
    rows, loads = dens.shape
    panels = rows // cl
    quarter = LANES // cl
    near = tiles.shape[0]
    vrows = cl * rank
    tile_cols = pl.ds(pl.multiple_of(k * LANES, LANES), LANES)
    wx = (1 - k) * ns + s
    wc = k * ns + 1 - s
    wd = (1 - k) * ns + 1 - s
    bdev = {"blk": 1 - k}
    cdev = {"sub": 1 - s}

    def rcopy(src, dst, ss, rs, dev):
        return pltpu.make_async_remote_copy(
            src_ref=src, dst_ref=dst, send_sem=ss, recv_sem=rs, device_id=dev,
            device_id_type=pl.DeviceIdType.MESH,
        )

    def zdev(t):
        return {"cluster": t}

    small = [
        pltpu.make_async_copy(a, b, loc_sem.at[6 + i])
        for i, (a, b) in enumerate(
            (
                (bucket_h, bucket_s), (cols_h, cols_s), (nrow_h, nrow_s), (ncol_h, ncol_s),
                (leaf_h, leaf), (normal_h, normal), (arm_h, arm), (area_h, area),
            )
        )
    ]
    for c in small[:4]:
        c.start()
    local = [
        pltpu.make_async_copy(far_v, vin, loc_sem.at[0]),
        pltpu.make_async_copy(dens.at[:, tile_cols], dv, loc_sem.at[1]),
        pltpu.make_async_copy(far_u, u_all.at[w], loc_sem.at[2]),
        pltpu.make_async_copy(tiles, nt.at[w], loc_sem.at[3]),
        pltpu.make_async_copy(grad, g_v, loc_sem.at[4]),
    ]
    for c in local + small[4:]:
        c.start()

    bar = pltpu.get_barrier_semaphore()

    def greet_z(d):
        pl.semaphore_signal(
            bar, inc=1, device_id=zdev(lax.rem(me + d + 1, nc)), device_id_type=pl.DeviceIdType.MESH
        )

    each(nc - 1, greet_z)
    mates = [(e, g) for e in range(nb) for g in range(ns) if (e, g) != (0, 0)]
    for e, g in mates:
        pl.semaphore_signal(
            bar, inc=1,
            device_id={"blk": lax.rem(k + e, nb), "sub": lax.rem(s + g, ns)},
            device_id_type=pl.DeviceIdType.MESH,
        )

    for c in small[:4]:
        c.wait()
    rid = lax.broadcasted_iota(jnp.int32, (8, LANES), 0)
    m = jnp.zeros((8, LANES), jnp.int32)
    for i in range(near):
        m = jnp.where(rid == i, ncol_s[i], m)
        m = jnp.where(rid == near + i, nrow_s[i], m)
    meta[pl.ds(w, 1)] = m.astype(F32)[None]

    local[0].wait()
    rr = lax.broadcasted_iota(jnp.int32, (rank, panels), 0)
    hr = lax.broadcasted_iota(jnp.int32, (16, panels), 0)

    def build(a):
        head = jnp.zeros((16, panels), jnp.int32)
        for q in range(cl):
            b = bucket_s[a * cl + q]
            width = jnp.where(b > 0, lax.shift_right_logical(jnp.int32(rank), 4 - b), 0)
            blk = vin[a * cl + q]
            vs[a, q * rank : (q + 1) * rank, :] = jnp.where(
                rr < width, blk.astype(F32), 0.0
            ).astype(BF16)
            head = jnp.where(hr == q, cols_s[a * cl + q], head)
        vs[a, vrows : vrows + 16, :] = head.astype(F32).astype(BF16)

    each(nc, build)


    lane = lax.broadcasted_iota(jnp.int32, (panels, LANES), 1)
    low = lane < quarter

    def roll(v):
        return pltpu.roll(v, quarter, 1)

    local[1].wait()
    d0 = dv[0:panels, :].astype(F32)
    d1 = dv[panels : 2 * panels, :].astype(F32)
    even = jnp.where(low, d0, roll(d1))
    odd = jnp.where(low, roll(d0), d1)
    sv = jnp.full((panels, LANES), s, jnp.int32)
    xg1[pl.ds(me, 1)] = jnp.where(sv == 0, even, odd).astype(BF16)[None]

    pl.semaphore_wait(bar, nc - 1 + len(mates))

    def x_send(i, xg, t):
        return rcopy(xg.at[me], xg.at[me], z_s.at[i, t], z_r.at[i, me], zdev(t))

    def x_recv(i, xg, c):
        return rcopy(xg.at[c], xg.at[c], z_s.at[i, c], z_r.at[i, c], zdev(c))

    def v_send(t):
        return rcopy(vs.at[t], vr.at[w, me], v_s.at[t], v_r.at[me], zdev(t))

    weights = ((far_u, u_all), (tiles, nt), (meta.at[w], meta))

    def w_x(j, p):
        src, dst = weights[j]
        return rcopy(src, dst.at[p], wx_s.at[j], wx_r.at[j], bdev)

    def w_c(j, i, p):
        src, dst = weights[j]
        return rcopy(src if i == 0 else dst.at[p], dst.at[p], wc_s.at[j, i], wc_r.at[j, i], cdev)

    def v_x(c, p):
        return rcopy(vr.at[p, c], vr.at[p, c], vx_s.at[c], vx_r.at[c], bdev)

    def v_c(i, c, p):
        return rcopy(vr.at[p, c], vr.at[p, c], vc_s.at[i, c], vc_r.at[i, c], cdev)

    vr[pl.ds(w, 1), pl.ds(me, 1)] = vs[pl.ds(me, 1)][None]
    each(nc - 1, lambda d: x_send(0, xg1, lax.rem(me + d + 1, nc)).start())
    each(nc - 1, lambda d: v_send(lax.rem(me + d + 1, nc)).start())
    for j in (2, 0, 1):
        w_x(j, w).start()
        w_c(j, 0, w).start()
    v_x(me, w).start()
    v_c(0, me, w).start()

    for c in small[4:]:
        c.wait()
    agrow[0:3, :] = normal[...]
    agrow[3:6, :] = arm[...]
    agrow[6:7, :] = area[...]
    agrow[7:8, :] = leaf[...].astype(F32)
    agcol[...] = jnp.transpose(agrow[...])

    def forward_v(d):
        c = lax.rem(me + nc - d - 1, nc)
        rcopy(vs.at[c], vr.at[w, c], v_s.at[c], v_r.at[c], zdev(c)).wait_recv()
        v_x(c, w).start()
        v_c(0, c, w).start()

    each(nc - 1, forward_v)
    for j in (2, 0, 1):
        w_x(j, wx).wait_recv()
        w_c(j, 1, wx).start()

    local[2].wait()
    local[3].wait()
    for j in range(3):
        w_c(j, 0, wc).wait_recv()
        w_c(j, 1, wd).wait_recv()
    for q in range(cl):
        for p in range(nb * ns):
            ut[q, p] = jnp.transpose(u_all[p, :, q].reshape(nc * rank, panels))

    def pass_v(d):
        c = lax.rem(me + nc - d, nc)
        v_x(c, wx).wait_recv()
        v_c(1, c, wx).start()

    each(nc, pass_v)

    def end_v(d):
        c = lax.rem(me + nc - d, nc)
        v_c(0, c, wc).wait_recv()
        v_c(1, c, wd).wait_recv()

    each(nc, end_v)

    lane_r = lax.broadcasted_iota(jnp.int32, (rank, LANES), 1)
    side = lane_r // quarter
    side_p = lane // quarter

    def apply(i, xg):
        for d in range(nc):
            c = lax.rem(me + nc - d, nc)
            if d > 0:
                x_recv(i, xg, c).wait_recv()
            for p in range(nb * ns):
                y = jnp.dot(vr[p, c, 0:vrows, :], xg[c], preferred_element_type=F32)
                yr = roll(y)
                h = vr[p, c, vrows : vrows + 16, 0:LANES].astype(F32)
                for q in range(cl):
                    r0 = q * rank
                    pick = jnp.where(
                        h[q : q + 1] == float(q), y[r0 : r0 + rank], yr[r0 : r0 + rank]
                    )
                    cf[q, p, c] = jnp.where(side == q, pick, 0.0).astype(BF16)
        acc = jnp.zeros((panels, LANES), F32)
        for q in range(cl):
            for p in range(nb * ns):
                acc = acc + jnp.dot(
                    ut[q, p], cf[q, p].reshape(nc * rank, LANES), preferred_element_type=F32
                )
        around = [xg[lax.rem(me + nc - 1 + j, nc)] for j in range(3)]
        for p in range(nb * ns):
            for n in range(near):
                col = meta[p, n : n + 1, :]
                row = meta[p, near + n : near + n + 1, :]
                chosen = jnp.zeros((panels, LANES), BF16)
                part = jnp.zeros((1, LANES), F32)
                for j in range(3):
                    hit = jnp.where((col >= float(j * cl)) & (col < float((j + 1) * cl)), 1.0, 0.0)
                    chosen = chosen + around[j] * hit.astype(BF16)
                    part = part + hit * (col - float(j * cl))
                val = jnp.dot(nt[p, n], chosen, preferred_element_type=F32)
                val = jnp.where(part == row, val, roll(val))
                acc = acc + jnp.where(side_p.astype(F32) == row, val, 0.0)
        return (0.5 * xg[me].astype(F32) + acc).astype(BF16)

    xg2[pl.ds(me, 1)] = apply(0, xg1)[None]
    each(nc - 1, lambda d: x_send(1, xg2, lax.rem(me + d + 1, nc)).start())
    pk[pl.ds(w, 1)] = apply(1, xg2)[None]

    def p_copy(idx, p):
        e, g = mates[idx]
        return rcopy(
            pk.at[p], pk.at[p], p_s.at[idx], p_r.at[idx],
            {"blk": lax.rem(k + e, nb), "sub": lax.rem(s + g, ns)},
        )

    for idx in range(len(mates)):
        p_copy(idx, w).start()
    for idx, (e, g) in enumerate(mates):
        p_copy(idx, lax.rem(k + nb - e, nb) * ns + lax.rem(s + ns - g, ns)).wait_recv()
    for kk in range(nb):
        e0 = pk[kk * ns].astype(F32)
        e1 = pk[kk * ns + 1].astype(F32)
        cols = slice(kk * LANES, (kk + 1) * LANES)
        pot[0:panels, cols] = jnp.where(low, e0, roll(e1)).astype(BF16)
        pot[panels : 2 * panels, cols] = jnp.where(low, roll(e0), e1).astype(BF16)
    pot_copy = pltpu.make_async_copy(pot, pot_out, loc_sem.at[5])
    pot_copy.start()

    local[4].wait()
    count = g_v.shape[1]
    step = 64

    def stress(gi, acc):
        g0 = pl.multiple_of(gi * step, step)
        cols = agcol[pl.ds(g0, step), :]
        n = [cols[:, j : j + 1] for j in range(3)]
        a = [cols[:, 3 + j : 4 + j] for j in range(3)]
        ar = cols[:, 6:7]
        lf = cols[:, 7:8]
        field = []
        for j in range(3):
            g = g_v[j, pl.ds(g0, step), :]
            fj = jnp.zeros((step, loads), F32)
            for q in range(cl):
                v = jnp.dot(g, pot[q * panels : (q + 1) * panels, :], preferred_element_type=F32)
                fj = jnp.where(lf == float(q), v, fj)
            field.append(fj)
        along = field[0] * n[0] + field[1] * n[1] + field[2] * n[2]
        sq = 0.5 * (field[0] * field[0] + field[1] * field[1] + field[2] * field[2])
        w = [(along * field[j] - sq * n[j]) * ar for j in range(3)]
        terms = []
        for q in range(cl):
            for j in range(3):
                terms.append(jnp.where(lf == float(q), w[j], 0.0))
        for j in range(3):
            x, y = (j + 1) % 3, (j + 2) % 3
            terms.append(a[x] * w[y] - a[y] * w[x])
        return tuple(
            o + jnp.sum(t.reshape(step // 8, 8, loads), axis=0) for o, t in zip(acc, terms)
        )

    nst = cl * 3 + 3
    zero = tuple(jnp.zeros((8, loads), F32) for _ in range(nst))
    sums = lax.fori_loop(0, count // step, stress, zero)
    for i in range(nst):
        stat[i : i + 1, :] = jnp.sum(sums[i], axis=0, keepdims=True)
    for idx, (e, g) in enumerate(mates):
        rcopy(
            stat, stat_r.at[idx], st_s.at[idx], st_r.at[idx],
            {"blk": lax.rem(k + e, nb), "sub": lax.rem(s + g, ns)},
        ).start()
    tot = stat[0:nst, :]
    for idx in range(len(mates)):
        rcopy(stat, stat_r.at[idx], st_s.at[idx], st_r.at[idx], cdev).wait_recv()
        tot = tot + stat_r[idx, 0:nst, :]
    tor_s[0:3, :] = tot[cl * 3 : cl * 3 + 3]

    def send_t(d):
        t = lax.rem(me + d + 1, nc)
        rcopy(tor_s, tor_r.at[d], t_s.at[d], t_r.at[d], zdev(t)).start()

    each(nc - 1, send_t)
    for q in range(cl):
        sec_out[q] = tot[q * 3 : q * 3 + 3]

    def wait_t(d):
        rcopy(tor_s, tor_r.at[d], t_s.at[d], t_r.at[d], zdev(me)).wait_recv()

    each(nc - 1, wait_t)
    if nc - 1 <= 4:
        tt = tor_s[0:3, :]
        for d in range(nc - 1):
            tt = tt + tor_r[d, 0:3, :]
    else:
        tt = lax.fori_loop(0, nc - 1, lambda d, t: t + tor_r[d, 0:3, :], tor_s[0:3, :])
    tor_out[...] = tt * scale

    def drain(d):
        t = lax.rem(me + d + 1, nc)
        x_send(0, xg1, t).wait_send()
        x_send(1, xg2, t).wait_send()
        v_send(t).wait_send()
        rcopy(tor_s, tor_r.at[d], t_s.at[d], t_r.at[d], zdev(t)).wait_send()

    each(nc - 1, drain)
    for c in range(nc):
        v_x(c, w).wait_send()
        v_c(0, c, w).wait_send()
        v_c(1, c, wx).wait_send()
    for j in range(3):
        w_x(j, w).wait_send()
        w_c(j, 0, w).wait_send()
        w_c(j, 1, wx).wait_send()
    for idx in range(len(mates)):
        p_copy(idx, w).wait_send()
        rcopy(stat, stat_r.at[idx], st_s.at[idx], st_r.at[idx], cdev).wait_send()
    pot_copy.wait()


def per_device(
    nc, nb, ns,
    density, far_cols, far_bucket, far_v, far_u, near_rows, near_cols, near_tiles,
    ag_leaf, ag_grad, ag_normal, ag_arm, ag_area,
):
    cl, panels, loads = density.shape
    rank = far_v.shape[1]
    near = near_tiles.shape[0]
    count = ag_leaf.shape[0]
    half = loads // ns
    rows = cl * panels
    ch = rows // nb
    vb = cl * rank + 16
    group = 4 if nc % 4 == 0 else nc
    scale = 1.0 / math.sqrt(nc * nb * ns)
    vm = pl.BlockSpec(memory_space=pltpu.VMEM)
    anyspace = pl.BlockSpec(memory_space=pl.ANY)
    dma = pltpu.SemaphoreType.DMA
    if nb == 2 and ns == 2 and cl == 2 and loads == 2 * LANES and nc <= 4:
        pot, sec, tor = pl.pallas_call(
            functools.partial(kernel4, nc, nb, ns, cl, rank, scale),
            out_shape=(
                jax.ShapeDtypeStruct((rows, loads), BF16),
                jax.ShapeDtypeStruct((cl, 3, loads), F32),
                jax.ShapeDtypeStruct((3, loads), F32),
            ),
            in_specs=[anyspace] * 13,
            out_specs=(anyspace, vm, vm),
            scratch_shapes=[
                pltpu.VMEM((nc * cl, rank, panels), BF16),
                pltpu.VMEM((nc, vb, panels), BF16),
                pltpu.VMEM((nb * ns, nc, vb, panels), BF16),
                pltpu.VMEM((nb * ns, nc, cl, rank, panels), BF16),
                pltpu.VMEM((cl, nb * ns, panels, nc * rank), BF16),
                pltpu.VMEM((nb * ns, near, panels, panels), BF16),
                pltpu.VMEM((nb * ns, 8, LANES), F32),
                pltpu.VMEM((3, count, panels), BF16),
                pltpu.VMEM((8, count), F32),
                pltpu.VMEM((count, 8), F32),
                pltpu.VMEM((rows, LANES), BF16),
                pltpu.VMEM((nc, panels, LANES), BF16),
                pltpu.VMEM((nc, panels, LANES), BF16),
                pltpu.VMEM((cl, nb * ns, nc, rank, LANES), BF16),
                pltpu.VMEM((nb * ns, panels, LANES), BF16),
                pltpu.VMEM((rows, loads), BF16),
                pltpu.VMEM((16, loads), F32),
                pltpu.VMEM((nb * ns - 1, 16, loads), F32),
                pltpu.VMEM((8, loads), F32),
                pltpu.VMEM((nc - 1, 8, loads), F32),
                pltpu.SMEM((nc * cl,), jnp.int32),
                pltpu.SMEM((nc * cl,), jnp.int32),
                pltpu.SMEM((near,), jnp.int32),
                pltpu.SMEM((near,), jnp.int32),
                pltpu.VMEM((1, count), jnp.int32),
                pltpu.VMEM((3, count), F32),
                pltpu.VMEM((3, count), F32),
                pltpu.VMEM((1, count), F32),
                dma((14,)), dma((3,)), dma((3,)), dma((3, 2)), dma((3, 2)),
                dma((nc,)), dma((nc,)), dma((nc,)), dma((nc,)), dma((2, nc)), dma((2, nc)),
                dma((2, nc)), dma((2, nc)),
                dma((nb * ns - 1,)), dma((nb * ns - 1,)),
                dma((nb * ns - 1,)), dma((nb * ns - 1,)),
                dma((nc - 1,)), dma((nc - 1,)),
            ],
            compiler_params=pltpu.CompilerParams(
                collective_id=0, has_side_effects=True, vmem_limit_bytes=63 * 1024 * 1024
            ),
        )(
            far_cols, far_bucket, near_rows, near_cols,
            density.reshape(rows, loads), far_v,
            far_u.reshape(nc, cl, rank, panels), near_tiles,
            ag_leaf.reshape(1, count), jnp.transpose(ag_grad, (1, 0, 2)),
            ag_normal, ag_arm, ag_area.reshape(1, count),
        )
    else:
        pot, sec, tor = pl.pallas_call(
            functools.partial(kernel, nc, nb, ns, cl, rank, scale),
            out_shape=(
                jax.ShapeDtypeStruct((rows, loads), BF16),
                jax.ShapeDtypeStruct((cl, 3, loads), F32),
                jax.ShapeDtypeStruct((3, loads), F32),
            ),
            in_specs=[anyspace] * 13,
            out_specs=(anyspace, vm, vm),
            scratch_shapes=[
                pltpu.VMEM((nc * cl, rank, panels), BF16),
                pltpu.VMEM((nc, vb, panels), BF16),
                pltpu.VMEM((ns, nc, vb, panels), BF16),
                pltpu.VMEM((nc, ns * cl * rank, cl * panels), BF16),
                pltpu.VMEM((ns, nc, cl, rank, panels), BF16),
                pltpu.VMEM((cl, ns * (nc // group), panels, group * rank), BF16),
                pltpu.VMEM((ns, near, panels, panels), BF16),
                pltpu.VMEM((ns, 8, LANES), F32),
                pltpu.VMEM((3, count, panels), BF16),
                pltpu.VMEM((8, count), F32),
                pltpu.VMEM((count, 8), F32),
                pltpu.VMEM((nc, rows, half), BF16),
                pltpu.VMEM((nc, rows, half), BF16),
                pltpu.VMEM((cl, ns, nc, rank, half), BF16),
                pltpu.VMEM((rows, half), F32),
                pltpu.VMEM((2, nb - 1, ch, half), BF16),
                pltpu.VMEM((2, nb - 1, ch, half), BF16),
                pltpu.VMEM((rows, loads), BF16),
                pltpu.VMEM((16, loads), F32),
                pltpu.VMEM((nb * ns - 1, 16, loads), F32),
                pltpu.VMEM((8, loads), F32),
                pltpu.VMEM((nc - 1, 8, loads), F32),
                pltpu.SMEM((nc * cl,), jnp.int32),
                pltpu.SMEM((nc * cl,), jnp.int32),
                pltpu.SMEM((near,), jnp.int32),
                pltpu.SMEM((near,), jnp.int32),
                pltpu.VMEM((1, count), jnp.int32),
                pltpu.VMEM((3, count), F32),
                pltpu.VMEM((3, count), F32),
                pltpu.VMEM((1, count), F32),
                dma((14,)), dma((3,)), dma((3,)),
                dma((nc,)), dma((nc,)), dma((nc,)), dma((nc,)),
                dma((2, nc)), dma((2, nc)), dma((2, nc, nb)), dma((2, nc, nb)),
                dma((2, nb - 1)), dma((2, nb - 1)),
                dma((nb,)), dma((nb,)), dma((nb,)), dma((nb,)),
                dma((nb * ns - 1,)), dma((nb * ns - 1,)),
                dma((nc - 1,)), dma((nc - 1,)),
            ],
            compiler_params=pltpu.CompilerParams(
                collective_id=0, has_side_effects=True, vmem_limit_bytes=63 * 1024 * 1024
            ),
        )(
            far_cols, far_bucket, near_rows, near_cols,
            density.reshape(rows, loads), far_v,
            far_u.reshape(nc, cl, rank, panels), near_tiles,
            ag_leaf.reshape(1, count), jnp.transpose(ag_grad, (1, 0, 2)),
            ag_normal, ag_arm, ag_area.reshape(1, count),
        )
    return pot.reshape(cl, panels, loads), sec, tor


def solution(mesh):
    placed = (
        P(("design", "cluster"), None, None),
        P(("design", "cluster", "blk", "sub")),
        P(("design", "cluster", "blk", "sub")),
        P(("design", "cluster", "blk", "sub"), None, None),
        P(("design", "cluster", "blk", "sub"), None, None),
        P(("design", "cluster", "blk", "sub")),
        P(("design", "cluster", "blk", "sub")),
        P(("design", "cluster", "blk", "sub"), None, None),
        P(("design", "cluster", "blk", "sub")),
        P(("design", "cluster", "blk", "sub"), None, None),
        P("design", ("cluster", "blk", "sub")),
        P("design", ("cluster", "blk", "sub")),
        P(("design", "cluster", "blk", "sub")),
    )
    sizes = tuple(mesh.shape[a] for a in ("cluster", "blk", "sub"))
    return jax.shard_map(
        functools.partial(per_device, *sizes),
        mesh=mesh,
        in_specs=placed,
        out_specs=(
            P(("design", "cluster"), None, None),
            P(("design", "cluster"), None, None),
            P("design", None),
        ),
        check_vma=False,
    )
```

```python
import functools
import math

import jax
import jax.numpy as jnp
from jax import lax
from jax.experimental import pallas as pl
from jax.experimental.pallas import tpu as pltpu
from jax.sharding import PartitionSpec as P

F32 = jnp.float32
BF16 = jnp.bfloat16
LANES = 128


def each(count, body):
    if count <= 4:
        for i in range(count):
            body(i)
    else:
        pl.loop(0, count)(body)


def kernel(
    nc, nb, ns, cl, rank, scale,
    cols_h, bucket_h, nrow_h, ncol_h,
    dens, far_v, far_u, tiles, leaf_h, grad, normal_h, arm_h, area_h,
    pot_out, sec_out, tor_out,
    vin, vs, vr, vx, u_all, ut, nt, meta, g_v, agrow, agcol, xg1, xg2, cf, part, rs_send, rs_recv,
    pot, stat, stat_r, tor_s, tor_r,
    cols_s, bucket_s, nrow_s, ncol_s, leaf, normal, arm, area,
    loc_sem, core_s, core_r, v_s, v_r, vc_s, vc_r,
    z_s, z_r, b_s, b_r, rs_s, rs_r, p_s, p_r, pc_s, pc_r, st_s, st_r, t_s, t_r,
):
    me = lax.axis_index("cluster")
    k = lax.axis_index("blk")
    s = lax.axis_index("sub")
    rows, loads = dens.shape
    panels = rows // cl
    half = loads // ns
    ch = rows // nb
    near = tiles.shape[0]
    vrows = cl * rank
    my_rows = pl.ds(pl.multiple_of(k * ch, ch), ch)
    my_cols = pl.ds(pl.multiple_of(s * half, half), half)
    other = 1 - s

    def rcopy(src, dst, ss, rs, dev):
        return pltpu.make_async_remote_copy(
            src_ref=src, dst_ref=dst, send_sem=ss, recv_sem=rs, device_id=dev,
            device_id_type=pl.DeviceIdType.MESH,
        )

    def zdev(t):
        return {"cluster": t}

    def bdev(t):
        return {"blk": t}

    cdev = {"sub": other}

    small = [
        pltpu.make_async_copy(a, b, loc_sem.at[6 + i])
        for i, (a, b) in enumerate(
            (
                (bucket_h, bucket_s), (cols_h, cols_s), (nrow_h, nrow_s), (ncol_h, ncol_s),
                (leaf_h, leaf), (normal_h, normal), (arm_h, arm), (area_h, area),
            )
        )
    ]
    for c in small[:4]:
        c.start()
    local = [
        pltpu.make_async_copy(far_v, vin, loc_sem.at[0]),
        pltpu.make_async_copy(dens.at[:, my_cols], xg1.at[me], loc_sem.at[1]),
        pltpu.make_async_copy(far_u, u_all.at[s], loc_sem.at[2]),
        pltpu.make_async_copy(tiles, nt.at[s], loc_sem.at[3]),
        pltpu.make_async_copy(grad, g_v, loc_sem.at[4]),
    ]
    for c in local + small[4:]:
        c.start()

    bar = pltpu.get_barrier_semaphore()

    def greet_z(d):
        pl.semaphore_signal(
            bar, inc=1, device_id=zdev(lax.rem(me + d + 1, nc)), device_id_type=pl.DeviceIdType.MESH
        )

    each(nc - 1, greet_z)
    mates = [(e, g) for e in range(nb) for g in range(ns) if (e, g) != (0, 0)]
    for e, g in mates:
        pl.semaphore_signal(
            bar, inc=1,
            device_id={"blk": lax.rem(k + e, nb), "sub": lax.rem(s + g, ns)},
            device_id_type=pl.DeviceIdType.MESH,
        )

    for c in small[:4]:
        c.wait()
    rid = lax.broadcasted_iota(jnp.int32, (8, LANES), 0)
    m = jnp.zeros((8, LANES), jnp.int32)
    for i in range(near):
        m = jnp.where(rid == i, ncol_s[i], m)
        m = jnp.where(rid == near + i, nrow_s[i], m)
    meta[pl.ds(s, 1)] = m.astype(F32)[None]

    local[0].wait()
    rr = lax.broadcasted_iota(jnp.int32, (rank, panels), 0)
    hr = lax.broadcasted_iota(jnp.int32, (16, panels), 0)

    def build(a):
        head = jnp.zeros((16, panels), jnp.int32)
        for q in range(cl):
            b = bucket_s[a * cl + q]
            width = jnp.where(b > 0, lax.shift_right_logical(jnp.int32(rank), 4 - b), 0)
            blk = vin[a * cl + q]
            vs[a, q * rank : (q + 1) * rank, :] = jnp.where(
                rr < width, blk.astype(F32), 0.0
            ).astype(BF16)
            head = jnp.where(hr == q, cols_s[a * cl + q], head)
        vs[a, vrows : vrows + 16, :] = head.astype(F32).astype(BF16)

    each(nc, build)

    pl.semaphore_wait(bar, nc - 1 + len(mates))

    def send_x1(d):
        t = lax.rem(me + d + 1, nc)
        rcopy(
            dens.at[my_rows, my_cols], xg1.at[me, my_rows], z_s.at[0, t], z_r.at[0, me], zdev(t)
        ).start()

    each(nc - 1, send_x1)

    def send_v(d):
        t = lax.rem(me + d + 1, nc)
        rcopy(vs.at[t], vr.at[s, me], v_s.at[t], v_r.at[me], zdev(t)).start()

    each(nc - 1, send_v)
    core = [
        rcopy(far_u, u_all.at[s], core_s.at[0], core_r.at[0], cdev),
        rcopy(tiles, nt.at[s], core_s.at[1], core_r.at[1], cdev),
        rcopy(meta.at[s], meta.at[s], core_s.at[2], core_r.at[2], cdev),
    ]
    for c in core:
        c.start()
    rcopy(vs.at[me], vr.at[s, me], vc_s.at[me], vc_r.at[me], cdev).start()

    for c in small[4:]:
        c.wait()
    agrow[0:3, :] = normal[...]
    agrow[3:6, :] = arm[...]
    agrow[6:7, :] = area[...]
    agrow[7:8, :] = leaf[...].astype(F32)
    agcol[...] = jnp.transpose(agrow[...])

    def forward_x(i, xg):
        def body(d):
            c = lax.rem(me + nc - d - 1, nc)
            rcopy(
                xg.at[c, my_rows], xg.at[c, my_rows], z_s.at[i, c], z_r.at[i, c], zdev(c)
            ).wait_recv()
            share(i, xg, c)

        each(nc - 1, body)

    def share(i, xg, c):
        for e in range(1, nb):
            t = lax.rem(k + e, nb)
            rcopy(
                xg.at[c, my_rows], xg.at[c, my_rows], b_s.at[i, c, t], b_r.at[i, c, k], bdev(t)
            ).start()

    def peer_rows(e):
        t = lax.rem(k + nb - e, nb)
        return t, pl.ds(pl.multiple_of(t * ch, ch), ch)

    def wait_shared(i, xg, c):
        for e in range(1, nb):
            t, pr = peer_rows(e)
            rcopy(
                xg.at[c, pr], xg.at[c, pr], b_s.at[i, c, t], b_r.at[i, c, t], bdev(t)
            ).wait_recv()

    forward_x(0, xg1)

    def forward_v(d):
        c = lax.rem(me + nc - d - 1, nc)
        rcopy(vs.at[c], vr.at[s, c], v_s.at[c], v_r.at[c], zdev(c)).wait_recv()
        rcopy(vr.at[s, c], vr.at[s, c], vc_s.at[c], vc_r.at[c], cdev).start()

    each(nc - 1, forward_v)

    local[2].wait()
    core[0].wait_recv()
    group = 4 if nc % 4 == 0 else nc

    for q in range(cl):
        for sp in range(ns):
            def turn(i, q=q, sp=sp):
                u = u_all[sp, pl.ds(i * group, group), q].reshape(group * rank, panels)
                ut[q, sp * (nc // group) + i] = jnp.transpose(u)

            each(nc // group, turn)

    vr[pl.ds(s, 1), pl.ds(me, 1)] = vs[pl.ds(me, 1)][None]

    def expand(d):
        c = lax.rem(me + nc - d, nc)
        rcopy(vs.at[c], vr.at[other, c], vc_s.at[c], vc_r.at[c], cdev).wait_recv()
        for sp in range(ns):
            for q in range(cl):
                v = vr[sp, c, q * rank : (q + 1) * rank, :]
                h = vr[sp, c, vrows : vrows + 16, :][q : q + 1]
                r0 = (sp * cl + q) * rank
                for j in range(cl):
                    w = jnp.where(h.astype(F32) == float(j), 1.0, 0.0).astype(BF16)
                    vx[c, r0 : r0 + rank, j * panels : (j + 1) * panels] = v * w

    each(nc, expand)

    local[1].wait()
    local[3].wait()
    core[1].wait_recv()
    core[2].wait_recv()

    def apply(i, xg):
        def coeff(d):
            c = lax.rem(me + nc - d, nc)
            if i == 0:
                if isinstance(d, int):
                    if d > 0:
                        wait_shared(i, xg, c)
                else:
                    pl.when(d > 0)(lambda: wait_shared(i, xg, c))
            else:
                wait_shared(i, xg, c)
            y = jnp.dot(vx[c], xg[c], preferred_element_type=F32).astype(BF16)
            for sp in range(ns):
                for q in range(cl):
                    r0 = (sp * cl + q) * rank
                    cf[q, sp, c] = y[r0 : r0 + rank]

        each(nc, coeff)
        acc = []
        for q in range(cl):
            total = jnp.zeros((panels, half), F32)
            for sp in range(ns):
                def far_step(gi, total, q=q, sp=sp):
                    w = cf[q, sp, pl.ds(gi * group, group)].reshape(group * rank, half)
                    return total + jnp.dot(
                        ut[q, sp * (nc // group) + gi], w, preferred_element_type=F32
                    )

                if nc == group:
                    total = far_step(0, total)
                else:
                    total = lax.fori_loop(0, nc // group, far_step, total)
            acc.append(total)
        for sp in range(ns):
            for n in range(near):
                col = meta[sp, n : n + 1, :]
                row = meta[sp, near + n : near + n + 1, :]
                chosen = jnp.zeros((panels, half), BF16)
                for j in range(3 * cl):
                    c = lax.rem(me + nc - 1 + j // cl, nc)
                    w = jnp.where(col == float(j), 1.0, 0.0).astype(BF16)
                    p0 = (j % cl) * panels
                    chosen = chosen + xg[c, p0 : p0 + panels, :] * w
                val = jnp.dot(nt[sp, n], chosen, preferred_element_type=F32)
                for q in range(cl):
                    acc[q] = acc[q] + jnp.where(row == float(q), val, 0.0)
        for q in range(cl):
            part[q * panels : (q + 1) * panels, :] = acc[q]
        for e in range(1, nb):
            t = lax.rem(k + e, nb)
            tr = pl.ds(pl.multiple_of(t * ch, ch), ch)
            rs_send[i, e - 1] = part[tr, :].astype(rs_send.dtype)
            rcopy(
                rs_send.at[i, e - 1], rs_recv.at[i, e - 1], rs_s.at[i, e - 1], rs_r.at[i, e - 1], bdev(t)
            ).start()
        out = part[my_rows, :]
        for e in range(1, nb):
            rcopy(
                rs_send.at[i, e - 1], rs_recv.at[i, e - 1], rs_s.at[i, e - 1], rs_r.at[i, e - 1], bdev(k)
            ).wait_recv()
            out = out + rs_recv[i, e - 1].astype(F32)
        return (0.5 * xg[me, my_rows, :].astype(F32) + out).astype(BF16)

    first = apply(0, xg1)
    xg2[me, my_rows, :] = first

    def send_x2(d):
        t = lax.rem(me + d + 1, nc)
        rcopy(
            xg2.at[me, my_rows], xg2.at[me, my_rows], z_s.at[1, t], z_r.at[1, me], zdev(t)
        ).start()

    each(nc - 1, send_x2)
    share(1, xg2, me)
    forward_x(1, xg2)
    potential = apply(1, xg2)

    pot[my_rows, my_cols] = potential
    for e in range(1, nb):
        t = lax.rem(k + e, nb)
        rcopy(
            pot.at[my_rows, my_cols], pot.at[my_rows, my_cols], p_s.at[t], p_r.at[k], bdev(t)
        ).start()
    rcopy(pot.at[my_rows, my_cols], pot.at[my_rows, my_cols], pc_s.at[k], pc_r.at[k], cdev).start()
    for e in range(1, nb):
        t, pr = peer_rows(e)
        rcopy(
            pot.at[pr, my_cols], pot.at[pr, my_cols], p_s.at[t], p_r.at[t], bdev(t)
        ).wait_recv()
        rcopy(pot.at[pr, my_cols], pot.at[pr, my_cols], pc_s.at[t], pc_r.at[t], cdev).start()
    oc = pl.ds(pl.multiple_of(other * half, half), half)
    for e in range(nb):
        t, pr = peer_rows(e)
        rcopy(pot.at[pr, oc], pot.at[pr, oc], pc_s.at[t], pc_r.at[t], cdev).wait_recv()
    pot_copy = pltpu.make_async_copy(pot, pot_out, loc_sem.at[5])
    pot_copy.start()

    local[4].wait()
    count = g_v.shape[1]
    step = 64

    def stress(gi, acc):
        g0 = pl.multiple_of(gi * step, step)
        cols = agcol[pl.ds(g0, step), :]
        n = [cols[:, j : j + 1] for j in range(3)]
        a = [cols[:, 3 + j : 4 + j] for j in range(3)]
        ar = cols[:, 6:7]
        lf = cols[:, 7:8]
        field = []
        for j in range(3):
            g = g_v[j, pl.ds(g0, step), :]
            fj = jnp.zeros((step, loads), F32)
            for q in range(cl):
                v = jnp.dot(g, pot[q * panels : (q + 1) * panels, :], preferred_element_type=F32)
                fj = jnp.where(lf == float(q), v, fj)
            field.append(fj)
        along = field[0] * n[0] + field[1] * n[1] + field[2] * n[2]
        sq = 0.5 * (field[0] * field[0] + field[1] * field[1] + field[2] * field[2])
        w = [(along * field[j] - sq * n[j]) * ar for j in range(3)]
        terms = []
        for q in range(cl):
            for j in range(3):
                terms.append(jnp.where(lf == float(q), w[j], 0.0))
        for j in range(3):
            x, y = (j + 1) % 3, (j + 2) % 3
            terms.append(a[x] * w[y] - a[y] * w[x])
        return tuple(
            o + jnp.sum(t.reshape(step // 8, 8, loads), axis=0) for o, t in zip(acc, terms)
        )

    nst = cl * 3 + 3
    zero = tuple(jnp.zeros((8, loads), F32) for _ in range(nst))
    sums = lax.fori_loop(0, count // step, stress, zero)
    for i in range(nst):
        stat[i : i + 1, :] = jnp.sum(sums[i], axis=0, keepdims=True)
    for idx, (e, g) in enumerate(mates):
        rcopy(
            stat, stat_r.at[idx], st_s.at[idx], st_r.at[idx],
            {"blk": lax.rem(k + e, nb), "sub": lax.rem(s + g, ns)},
        ).start()
    tot = stat[0:nst, :]
    for idx in range(len(mates)):
        rcopy(stat, stat_r.at[idx], st_s.at[idx], st_r.at[idx], cdev).wait_recv()
        tot = tot + stat_r[idx, 0:nst, :]
    tor_s[0:3, :] = tot[cl * 3 : cl * 3 + 3]

    def send_t(d):
        t = lax.rem(me + d + 1, nc)
        rcopy(tor_s, tor_r.at[d], t_s.at[d], t_r.at[d], zdev(t)).start()

    each(nc - 1, send_t)
    for q in range(cl):
        sec_out[q] = tot[q * 3 : q * 3 + 3]

    def wait_t(d):
        rcopy(tor_s, tor_r.at[d], t_s.at[d], t_r.at[d], zdev(me)).wait_recv()

    each(nc - 1, wait_t)
    if nc - 1 <= 4:
        tt = tor_s[0:3, :]
        for d in range(nc - 1):
            tt = tt + tor_r[d, 0:3, :]
    else:
        tt = lax.fori_loop(0, nc - 1, lambda d, t: t + tor_r[d, 0:3, :], tor_s[0:3, :])
    tor_out[...] = tt * scale

    def drain_z(d):
        t = lax.rem(me + d + 1, nc)
        rcopy(
            dens.at[my_rows, my_cols], xg1.at[me, my_rows], z_s.at[0, t], z_r.at[0, me], zdev(t)
        ).wait_send()
        rcopy(vs.at[t], vr.at[s, me], v_s.at[t], v_r.at[me], zdev(t)).wait_send()
        rcopy(
            xg2.at[me, my_rows], xg2.at[me, my_rows], z_s.at[1, t], z_r.at[1, me], zdev(t)
        ).wait_send()
        rcopy(tor_s, tor_r.at[d], t_s.at[d], t_r.at[d], zdev(t)).wait_send()
        rcopy(vr.at[s, t], vr.at[s, t], vc_s.at[t], vc_r.at[t], cdev).wait_send()
        for e in range(1, nb):
            b = lax.rem(k + e, nb)
            for i, xg in ((0, xg1), (1, xg2)):
                rcopy(
                    xg.at[t, my_rows], xg.at[t, my_rows], b_s.at[i, t, b], b_r.at[i, t, k], bdev(b)
                ).wait_send()

    each(nc - 1, drain_z)
    rcopy(vs.at[me], vr.at[s, me], vc_s.at[me], vc_r.at[me], cdev).wait_send()
    for c in core:
        c.wait_send()
    for e in range(1, nb):
        b = lax.rem(k + e, nb)
        rcopy(
            xg2.at[me, my_rows], xg2.at[me, my_rows], b_s.at[1, me, b], b_r.at[1, me, k], bdev(b)
        ).wait_send()
        for i in range(2):
            rcopy(
                rs_send.at[i, e - 1], rs_recv.at[i, e - 1], rs_s.at[i, e - 1], rs_r.at[i, e - 1], bdev(b)
            ).wait_send()
        rcopy(
            pot.at[my_rows, my_cols], pot.at[my_rows, my_cols], p_s.at[b], p_r.at[k], bdev(b)
        ).wait_send()
    for e in range(nb):
        t, pr = peer_rows(e)
        rcopy(pot.at[pr, my_cols], pot.at[pr, my_cols], pc_s.at[t], pc_r.at[t], cdev).wait_send()
    for idx in range(len(mates)):
        rcopy(stat, stat_r.at[idx], st_s.at[idx], st_r.at[idx], cdev).wait_send()
    pot_copy.wait()


def kernel4(
    nc, nb, ns, cl, rank, scale,
    cols_h, bucket_h, nrow_h, ncol_h,
    dens, far_v, far_u, tiles, leaf_h, grad, normal_h, arm_h, area_h,
    pot_out, sec_out, tor_out,
    vin, vs, vr, u_all, ut, nt, meta, g_v, agrow, agcol, dv, xg1, xg2, cf, pk,
    pot, stat, stat_r, tor_s, tor_r, tor_a,
    cols_s, bucket_s, nrow_s, ncol_s, leaf, normal, arm, area,
    loc_sem, wx_s, wx_r, wc_s, wc_r, v_s, v_r, vx_s, vx_r, vc_s, vc_r,
    z_s, z_r, p_s, p_r, st_s, st_r, t_s, t_r,
):
    me = lax.axis_index("cluster")
    k = lax.axis_index("blk")
    s = lax.axis_index("sub")
    w = k * ns + s
    rows, loads = dens.shape
    panels = rows // cl
    quarter = LANES // cl
    near = tiles.shape[0]
    vrows = cl * rank
    tile_cols = pl.ds(pl.multiple_of(k * LANES, LANES), LANES)
    wx = (1 - k) * ns + s
    wc = k * ns + 1 - s
    wd = (1 - k) * ns + 1 - s
    bdev = {"blk": 1 - k}
    cdev = {"sub": 1 - s}

    def rcopy(src, dst, ss, rs, dev):
        return pltpu.make_async_remote_copy(
            src_ref=src, dst_ref=dst, send_sem=ss, recv_sem=rs, device_id=dev,
            device_id_type=pl.DeviceIdType.MESH,
        )

    def zdev(t):
        return {"cluster": t}

    small = [
        pltpu.make_async_copy(a, b, loc_sem.at[6 + i])
        for i, (a, b) in enumerate(
            (
                (bucket_h, bucket_s), (cols_h, cols_s), (nrow_h, nrow_s), (ncol_h, ncol_s),
                (leaf_h, leaf), (normal_h, normal), (arm_h, arm), (area_h, area),
            )
        )
    ]
    for c in small[:4]:
        c.start()
    local = [
        pltpu.make_async_copy(far_v, vin, loc_sem.at[0]),
        pltpu.make_async_copy(dens.at[:, tile_cols], dv, loc_sem.at[1]),
        pltpu.make_async_copy(far_u, u_all.at[w], loc_sem.at[2]),
        pltpu.make_async_copy(tiles, nt.at[w], loc_sem.at[3]),
        pltpu.make_async_copy(grad, g_v, loc_sem.at[4]),
    ]
    for c in local + small[4:]:
        c.start()

    bar = pltpu.get_barrier_semaphore()

    mates = [(e, g) for e in range(nb) for g in range(ns) if (e, g) != (0, 0)]
    everyone = [
        (d, e, g) for d in range(nc) for e in range(nb) for g in range(ns) if (d, e, g) != (0, 0, 0)
    ]

    def at(d, e, g):
        return {
            "cluster": lax.rem(me + d, nc),
            "blk": lax.rem(k + e, nb),
            "sub": lax.rem(s + g, ns),
        }

    for there in everyone:
        pl.semaphore_signal(
            bar, inc=1, device_id=at(*there), device_id_type=pl.DeviceIdType.MESH
        )

    for c in small[:4]:
        c.wait()
    rid = lax.broadcasted_iota(jnp.int32, (8, LANES), 0)
    m = jnp.zeros((8, LANES), jnp.int32)
    for i in range(near):
        m = jnp.where(rid == i, ncol_s[i], m)
        m = jnp.where(rid == near + i, nrow_s[i], m)
    meta[pl.ds(w, 1)] = m.astype(F32)[None]

    local[0].wait()
    rr = lax.broadcasted_iota(jnp.int32, (rank, panels), 0)
    hr = lax.broadcasted_iota(jnp.int32, (16, panels), 0)

    def build(a):
        head = jnp.zeros((16, panels), jnp.int32)
        for q in range(cl):
            b = bucket_s[a * cl + q]
            width = jnp.where(b > 0, lax.shift_right_logical(jnp.int32(rank), 4 - b), 0)
            blk = vin[a * cl + q]
            vs[a, q * rank : (q + 1) * rank, :] = jnp.where(
                rr < width, blk.astype(F32), 0.0
            ).astype(BF16)
            head = jnp.where(hr == q, cols_s[a * cl + q], head)
        vs[a, vrows : vrows + 16, :] = head.astype(F32).astype(BF16)

    each(nc, build)


    lane = lax.broadcasted_iota(jnp.int32, (panels, LANES), 1)
    low = lane < quarter

    def roll(v):
        return pltpu.roll(v, quarter, 1)

    local[1].wait()
    d0 = dv[0:panels, :].astype(F32)
    d1 = dv[panels : 2 * panels, :].astype(F32)
    even = jnp.where(low, d0, roll(d1))
    odd = jnp.where(low, roll(d0), d1)
    sv = jnp.full((panels, LANES), s, jnp.int32)
    xg1[pl.ds(me, 1)] = jnp.where(sv == 0, even, odd).astype(BF16)[None]

    pl.semaphore_wait(bar, len(everyone))

    def x_send(i, xg, t):
        return rcopy(xg.at[me], xg.at[me], z_s.at[i, t], z_r.at[i, me], zdev(t))

    def x_recv(i, xg, c):
        return rcopy(xg.at[c], xg.at[c], z_s.at[i, c], z_r.at[i, c], zdev(c))

    def v_send(t):
        return rcopy(vs.at[t], vr.at[w, me], v_s.at[t], v_r.at[me], zdev(t))

    weights = ((far_u, u_all), (tiles, nt), (meta.at[w], meta))

    def w_x(j, p):
        src, dst = weights[j]
        return rcopy(src, dst.at[p], wx_s.at[j], wx_r.at[j], bdev)

    def w_c(j, i, p):
        src, dst = weights[j]
        return rcopy(src if i == 0 else dst.at[p], dst.at[p], wc_s.at[j, i], wc_r.at[j, i], cdev)

    def v_x(c, p):
        return rcopy(vr.at[p, c], vr.at[p, c], vx_s.at[c], vx_r.at[c], bdev)

    def v_c(i, c, p):
        return rcopy(vr.at[p, c], vr.at[p, c], vc_s.at[i, c], vc_r.at[i, c], cdev)

    vr[pl.ds(w, 1), pl.ds(me, 1)] = vs[pl.ds(me, 1)][None]
    each(nc - 1, lambda d: x_send(0, xg1, lax.rem(me + d + 1, nc)).start())
    each(nc - 1, lambda d: v_send(lax.rem(me + d + 1, nc)).start())
    for j in (2, 0, 1):
        w_x(j, w).start()
        w_c(j, 0, w).start()
    v_x(me, w).start()
    v_c(0, me, w).start()

    for c in small[4:]:
        c.wait()
    agrow[0:3, :] = normal[...]
    agrow[3:6, :] = arm[...]
    agrow[6:7, :] = area[...]
    agrow[7:8, :] = leaf[...].astype(F32)
    agcol[...] = jnp.transpose(agrow[...])

    def forward_v(d):
        c = lax.rem(me + nc - d - 1, nc)
        rcopy(vs.at[c], vr.at[w, c], v_s.at[c], v_r.at[c], zdev(c)).wait_recv()
        v_x(c, w).start()
        v_c(0, c, w).start()

    each(nc - 1, forward_v)
    for j in (2, 0, 1):
        w_x(j, wx).wait_recv()
        w_c(j, 1, wx).start()

    local[2].wait()
    local[3].wait()
    for j in range(3):
        w_c(j, 0, wc).wait_recv()
        w_c(j, 1, wd).wait_recv()
    for q in range(cl):
        for p in range(nb * ns):
            ut[q, p] = jnp.transpose(u_all[p, :, q].reshape(nc * rank, panels))

    def pass_v(d):
        c = lax.rem(me + nc - d, nc)
        v_x(c, wx).wait_recv()
        v_c(1, c, wx).start()

    each(nc, pass_v)

    def end_v(d):
        c = lax.rem(me + nc - d, nc)
        v_c(0, c, wc).wait_recv()
        v_c(1, c, wd).wait_recv()

    each(nc, end_v)

    lane_r = lax.broadcasted_iota(jnp.int32, (rank, LANES), 1)
    side = lane_r // quarter
    side_p = lane // quarter

    def apply(i, xg):
        for d in range(nc):
            c = lax.rem(me + nc - d, nc)
            if d > 0:
                x_recv(i, xg, c).wait_recv()
            for p in range(nb * ns):
                y = jnp.dot(vr[p, c, 0:vrows, :], xg[c], preferred_element_type=F32)
                yr = roll(y)
                h = vr[p, c, vrows : vrows + 16, 0:LANES].astype(F32)
                for q in range(cl):
                    r0 = q * rank
                    pick = jnp.where(
                        h[q : q + 1] == float(q), y[r0 : r0 + rank], yr[r0 : r0 + rank]
                    )
                    cf[q, p, c] = jnp.where(side == q, pick, 0.0).astype(BF16)
        acc = jnp.zeros((panels, LANES), F32)
        for q in range(cl):
            for p in range(nb * ns):
                acc = acc + jnp.dot(
                    ut[q, p], cf[q, p].reshape(nc * rank, LANES), preferred_element_type=F32
                )
        around = [xg[lax.rem(me + nc - 1 + j, nc)] for j in range(3)]
        for p in range(nb * ns):
            for n in range(near):
                col = meta[p, n : n + 1, :]
                row = meta[p, near + n : near + n + 1, :]
                chosen = jnp.zeros((panels, LANES), BF16)
                part = jnp.zeros((1, LANES), F32)
                for j in range(3):
                    hit = jnp.where((col >= float(j * cl)) & (col < float((j + 1) * cl)), 1.0, 0.0)
                    chosen = chosen + around[j] * hit.astype(BF16)
                    part = part + hit * (col - float(j * cl))
                val = jnp.dot(nt[p, n], chosen, preferred_element_type=F32)
                val = jnp.where(part == row, val, roll(val))
                acc = acc + jnp.where(side_p.astype(F32) == row, val, 0.0)
        return (0.5 * xg[me].astype(F32) + acc).astype(BF16)

    xg2[pl.ds(me, 1)] = apply(0, xg1)[None]
    each(nc - 1, lambda d: x_send(1, xg2, lax.rem(me + d + 1, nc)).start())
    pk[pl.ds(w, 1)] = apply(1, xg2)[None]

    def p_copy(idx, p):
        e, g = mates[idx]
        return rcopy(
            pk.at[p], pk.at[p], p_s.at[idx], p_r.at[idx],
            {"blk": lax.rem(k + e, nb), "sub": lax.rem(s + g, ns)},
        )

    for idx in range(len(mates)):
        p_copy(idx, w).start()
    for idx, (e, g) in enumerate(mates):
        p_copy(idx, lax.rem(k + nb - e, nb) * ns + lax.rem(s + ns - g, ns)).wait_recv()
    for kk in range(nb):
        e0 = pk[kk * ns].astype(F32)
        e1 = pk[kk * ns + 1].astype(F32)
        cols = slice(kk * LANES, (kk + 1) * LANES)
        pot[0:panels, cols] = jnp.where(low, e0, roll(e1)).astype(BF16)
        pot[panels : 2 * panels, cols] = jnp.where(low, roll(e0), e1).astype(BF16)
    pot_copy = pltpu.make_async_copy(pot, pot_out, loc_sem.at[5])
    pot_copy.start()

    local[4].wait()
    count = g_v.shape[1]
    step = 64

    def stress(gi, acc):
        g0 = pl.multiple_of(gi * step, step)
        cols = agcol[pl.ds(g0, step), :]
        n = [cols[:, j : j + 1] for j in range(3)]
        a = [cols[:, 3 + j : 4 + j] for j in range(3)]
        ar = cols[:, 6:7]
        lf = cols[:, 7:8]
        field = []
        for j in range(3):
            g = g_v[j, pl.ds(g0, step), :]
            fj = jnp.zeros((step, loads), F32)
            for q in range(cl):
                v = jnp.dot(g, pot[q * panels : (q + 1) * panels, :], preferred_element_type=F32)
                fj = jnp.where(lf == float(q), v, fj)
            field.append(fj)
        along = field[0] * n[0] + field[1] * n[1] + field[2] * n[2]
        sq = 0.5 * (field[0] * field[0] + field[1] * field[1] + field[2] * field[2])
        w = [(along * field[j] - sq * n[j]) * ar for j in range(3)]
        terms = []
        for q in range(cl):
            for j in range(3):
                terms.append(jnp.where(lf == float(q), w[j], 0.0))
        for j in range(3):
            x, y = (j + 1) % 3, (j + 2) % 3
            terms.append(a[x] * w[y] - a[y] * w[x])
        return tuple(
            o + jnp.sum(t.reshape(step // 8, 8, loads), axis=0) for o, t in zip(acc, terms)
        )

    nst = cl * 3 + 3
    zero = tuple(jnp.zeros((8, loads), F32) for _ in range(nst))
    sums = lax.fori_loop(0, count // step, stress, zero)
    for i in range(3):
        tor_s[i : i + 1, :] = jnp.sum(sums[cl * 3 + i], axis=0, keepdims=True)

    def t_copy(idx):
        return rcopy(tor_s, tor_r.at[idx], t_s.at[idx], t_r.at[idx], at(*everyone[idx]))

    for idx in range(len(everyone)):
        t_copy(idx).start()
    for i in range(cl * 3):
        stat[i : i + 1, :] = jnp.sum(sums[i], axis=0, keepdims=True)
    for idx, (e, g) in enumerate(mates):
        rcopy(stat, stat_r.at[idx], st_s.at[idx], st_r.at[idx], at(0, e, g)).start()
    tot = stat[...]
    for idx in range(len(mates)):
        rcopy(stat, stat_r.at[idx], st_s.at[idx], st_r.at[idx], cdev).wait_recv()
        tot = tot + stat_r[idx]
    for q in range(cl):
        for j in range(3):
            sec_out[j, q : q + 1, :] = tot[q * 3 + j : q * 3 + j + 1]
    mine = (me * nb + k) * ns + s
    slots = tor_a
    slots[pl.ds(mine, 1)] = tor_s[...][None]
    for idx, (d, e, g) in enumerate(everyone):
        t_copy(idx).wait_recv()
        who = (
            lax.rem(me + nc - d, nc) * nb + lax.rem(k + nb - e, nb)
        ) * ns + lax.rem(s + ns - g, ns)
        slots[pl.ds(who, 1)] = tor_r[idx][None]
    tt = slots[0, 0:3, :]
    for i in range(1, nc * nb * ns):
        tt = tt + slots[i, 0:3, :]
    tor_out[...] = tt * scale

    def drain(d):
        t = lax.rem(me + d + 1, nc)
        x_send(0, xg1, t).wait_send()
        x_send(1, xg2, t).wait_send()
        v_send(t).wait_send()

    each(nc - 1, drain)
    for c in range(nc):
        v_x(c, w).wait_send()
        v_c(0, c, w).wait_send()
        v_c(1, c, wx).wait_send()
    for j in range(3):
        w_x(j, w).wait_send()
        w_c(j, 0, w).wait_send()
        w_c(j, 1, wx).wait_send()
    for idx in range(len(mates)):
        p_copy(idx, w).wait_send()
        rcopy(stat, stat_r.at[idx], st_s.at[idx], st_r.at[idx], cdev).wait_send()
    for idx in range(len(everyone)):
        t_copy(idx).wait_send()
    pot_copy.wait()


def per_device(
    nc, nb, ns,
    density, far_cols, far_bucket, far_v, far_u, near_rows, near_cols, near_tiles,
    ag_leaf, ag_grad, ag_normal, ag_arm, ag_area,
):
    cl, panels, loads = density.shape
    rank = far_v.shape[1]
    near = near_tiles.shape[0]
    count = ag_leaf.shape[0]
    half = loads // ns
    rows = cl * panels
    ch = rows // nb
    vb = cl * rank + 16
    group = 4 if nc % 4 == 0 else nc
    scale = 1.0 / math.sqrt(nc * nb * ns)
    vm = pl.BlockSpec(memory_space=pltpu.VMEM)
    anyspace = pl.BlockSpec(memory_space=pl.ANY)
    dma = pltpu.SemaphoreType.DMA
    if nb == 2 and ns == 2 and cl == 2 and loads == 2 * LANES and nc <= 4:
        pot, sec, tor = pl.pallas_call(
            functools.partial(kernel4, nc, nb, ns, cl, rank, scale),
            out_shape=(
                jax.ShapeDtypeStruct((rows, loads), BF16),
                jax.ShapeDtypeStruct((3, cl, loads), F32),
                jax.ShapeDtypeStruct((3, loads), F32),
            ),
            in_specs=[anyspace] * 13,
            out_specs=(anyspace, vm, vm),
            scratch_shapes=[
                pltpu.VMEM((nc * cl, rank, panels), BF16),
                pltpu.VMEM((nc, vb, panels), BF16),
                pltpu.VMEM((nb * ns, nc, vb, panels), BF16),
                pltpu.VMEM((nb * ns, nc, cl, rank, panels), BF16),
                pltpu.VMEM((cl, nb * ns, panels, nc * rank), BF16),
                pltpu.VMEM((nb * ns, near, panels, panels), BF16),
                pltpu.VMEM((nb * ns, 8, LANES), F32),
                pltpu.VMEM((3, count, panels), BF16),
                pltpu.VMEM((8, count), F32),
                pltpu.VMEM((count, 8), F32),
                pltpu.VMEM((rows, LANES), BF16),
                pltpu.VMEM((nc, panels, LANES), BF16),
                pltpu.VMEM((nc, panels, LANES), BF16),
                pltpu.VMEM((cl, nb * ns, nc, rank, LANES), BF16),
                pltpu.VMEM((nb * ns, panels, LANES), BF16),
                pltpu.VMEM((rows, loads), BF16),
                pltpu.VMEM((8, loads), F32),
                pltpu.VMEM((nb * ns - 1, 8, loads), F32),
                pltpu.VMEM((8, loads), F32),
                pltpu.VMEM((nc * nb * ns - 1, 8, loads), F32),
                pltpu.VMEM((nc * nb * ns, 8, loads), F32),
                pltpu.SMEM((nc * cl,), jnp.int32),
                pltpu.SMEM((nc * cl,), jnp.int32),
                pltpu.SMEM((near,), jnp.int32),
                pltpu.SMEM((near,), jnp.int32),
                pltpu.VMEM((1, count), jnp.int32),
                pltpu.VMEM((3, count), F32),
                pltpu.VMEM((3, count), F32),
                pltpu.VMEM((1, count), F32),
                dma((14,)), dma((3,)), dma((3,)), dma((3, 2)), dma((3, 2)),
                dma((nc,)), dma((nc,)), dma((nc,)), dma((nc,)), dma((2, nc)), dma((2, nc)),
                dma((2, nc)), dma((2, nc)),
                dma((nb * ns - 1,)), dma((nb * ns - 1,)),
                dma((nb * ns - 1,)), dma((nb * ns - 1,)),
                dma((nc * nb * ns - 1,)), dma((nc * nb * ns - 1,)),
            ],
            compiler_params=pltpu.CompilerParams(
                collective_id=0, has_side_effects=True, vmem_limit_bytes=63 * 1024 * 1024
            ),
        )(
            far_cols, far_bucket, near_rows, near_cols,
            density.reshape(rows, loads), far_v,
            far_u.reshape(nc, cl, rank, panels), near_tiles,
            ag_leaf.reshape(1, count), jnp.transpose(ag_grad, (1, 0, 2)),
            ag_normal, ag_arm, ag_area.reshape(1, count),
        )
        sec = jnp.transpose(sec, (1, 0, 2))
    else:
        pot, sec, tor = pl.pallas_call(
            functools.partial(kernel, nc, nb, ns, cl, rank, scale),
            out_shape=(
                jax.ShapeDtypeStruct((rows, loads), BF16),
                jax.ShapeDtypeStruct((cl, 3, loads), F32),
                jax.ShapeDtypeStruct((3, loads), F32),
            ),
            in_specs=[anyspace] * 13,
            out_specs=(anyspace, vm, vm),
            scratch_shapes=[
                pltpu.VMEM((nc * cl, rank, panels), BF16),
                pltpu.VMEM((nc, vb, panels), BF16),
                pltpu.VMEM((ns, nc, vb, panels), BF16),
                pltpu.VMEM((nc, ns * cl * rank, cl * panels), BF16),
                pltpu.VMEM((ns, nc, cl, rank, panels), BF16),
                pltpu.VMEM((cl, ns * (nc // group), panels, group * rank), BF16),
                pltpu.VMEM((ns, near, panels, panels), BF16),
                pltpu.VMEM((ns, 8, LANES), F32),
                pltpu.VMEM((3, count, panels), BF16),
                pltpu.VMEM((8, count), F32),
                pltpu.VMEM((count, 8), F32),
                pltpu.VMEM((nc, rows, half), BF16),
                pltpu.VMEM((nc, rows, half), BF16),
                pltpu.VMEM((cl, ns, nc, rank, half), BF16),
                pltpu.VMEM((rows, half), F32),
                pltpu.VMEM((2, nb - 1, ch, half), BF16),
                pltpu.VMEM((2, nb - 1, ch, half), BF16),
                pltpu.VMEM((rows, loads), BF16),
                pltpu.VMEM((16, loads), F32),
                pltpu.VMEM((nb * ns - 1, 16, loads), F32),
                pltpu.VMEM((8, loads), F32),
                pltpu.VMEM((nc - 1, 8, loads), F32),
                pltpu.SMEM((nc * cl,), jnp.int32),
                pltpu.SMEM((nc * cl,), jnp.int32),
                pltpu.SMEM((near,), jnp.int32),
                pltpu.SMEM((near,), jnp.int32),
                pltpu.VMEM((1, count), jnp.int32),
                pltpu.VMEM((3, count), F32),
                pltpu.VMEM((3, count), F32),
                pltpu.VMEM((1, count), F32),
                dma((14,)), dma((3,)), dma((3,)),
                dma((nc,)), dma((nc,)), dma((nc,)), dma((nc,)),
                dma((2, nc)), dma((2, nc)), dma((2, nc, nb)), dma((2, nc, nb)),
                dma((2, nb - 1)), dma((2, nb - 1)),
                dma((nb,)), dma((nb,)), dma((nb,)), dma((nb,)),
                dma((nb * ns - 1,)), dma((nb * ns - 1,)),
                dma((nc - 1,)), dma((nc - 1,)),
            ],
            compiler_params=pltpu.CompilerParams(
                collective_id=0, has_side_effects=True, vmem_limit_bytes=63 * 1024 * 1024
            ),
        )(
            far_cols, far_bucket, near_rows, near_cols,
            density.reshape(rows, loads), far_v,
            far_u.reshape(nc, cl, rank, panels), near_tiles,
            ag_leaf.reshape(1, count), jnp.transpose(ag_grad, (1, 0, 2)),
            ag_normal, ag_arm, ag_area.reshape(1, count),
        )
    return pot.reshape(cl, panels, loads), sec, tor


def solution(mesh):
    placed = (
        P(("design", "cluster"), None, None),
        P(("design", "cluster", "blk", "sub")),
        P(("design", "cluster", "blk", "sub")),
        P(("design", "cluster", "blk", "sub"), None, None),
        P(("design", "cluster", "blk", "sub"), None, None),
        P(("design", "cluster", "blk", "sub")),
        P(("design", "cluster", "blk", "sub")),
        P(("design", "cluster", "blk", "sub"), None, None),
        P(("design", "cluster", "blk", "sub")),
        P(("design", "cluster", "blk", "sub"), None, None),
        P("design", ("cluster", "blk", "sub")),
        P("design", ("cluster", "blk", "sub")),
        P(("design", "cluster", "blk", "sub")),
    )
    sizes = tuple(mesh.shape[a] for a in ("cluster", "blk", "sub"))
    return jax.shard_map(
        functools.partial(per_device, *sizes),
        mesh=mesh,
        in_specs=placed,
        out_specs=(
            P(("design", "cluster"), None, None),
            P(("design", "cluster"), None, None),
            P("design", None),
        ),
        check_vma=False,
    )
```
